1024 devices in a mesh: row: 16 (over y, core), col: 64 (over z, x).
Axes of the slice: x: 8, y: 8, z: 8, core: 2. Of those that a mesh axis runs over, the one named last changes fastest.
Arguments:
- atm_flux: float32 [20, 98304], P(None, ('row', 'col')), may hold values from -6 to 6
- send_index: int32 [1024, 3, 3, 48], P(('row', 'col')), may hold values from 0 to 95
- send_count: int32 [1024, 3, 3], P(('row', 'col')), may hold values from 12 to 48, as said below
- block_start: int32 [1024, 3, 3, 48], P(('row', 'col')), may hold values from 0 to 1136, as said below
- remap_weight: float32 [1024, 3, 3, 48, 128], P(('row', 'col')), may hold values from 0.002 to 0.03
- coupling: float32 [8, 20], replicated, may hold values from -1.25 to 1.25
- ocean_state: float32 [8, 256, 8192], P(None, 'row', 'col'), may hold values from -6 to 6
- velocity: float32 [2, 256, 8192], P(None, 'row', 'col'), may hold values from -0.5 to 0.5
- diffusivity: float32 [8], replicated, may hold values from 0.02 to 0.2
- wet_mask: int32 [256, 8192], P('row', 'col'), may hold values 0 or 1
Outputs:
- new_state: float32 [8, 256, 8192], P(None, 'row', 'col')
- atm_surface: float32 [8, 98304], P(None, ('row', 'col'))
The draws below stay inside these ranges and needn't reach their ends.
Inputs may be any that keep to these rules, and one draw needn't show every extreme that they name: `send_count`: for every device the centre entry [d, 1, 1] is 48. `block_start`: each entry is y * 128 + x with 0 <= y <= 8 and 0 <= x <= 112, so that a slot's block of 8 x 16 cells lies inside the tile.
All inputs are finite; a program needn't handle non-finite values. No bound on the sum of `wet_mask` on one device may be relied on, other than what follows from the above.
Results may differ from the reference program's by a relative error of at most 0.00009.
Values sent between devices are 32-bit elements; how exact they have to be, the bound alone decides.
No kernel may reach another device: no remote copies, remote signals or barrier semaphores. Data moves between devices by JAX's collectives and lax.ppermute only.
A program may use at most 32 MiB of HBM per device.

```python
import math
import jax
import jax.numpy as jnp
from jax import lax

FIELDS = 20
OFIELDS = 8
A_DEV = 96
S = 48
WIN_R = 8
WIN_C = 16
WB = 128
OY = 16
OX = 128
O_CELLS = 2048
ATM_CELLS = 98304
NY = 256
NX = 8192
N_ROW = 16
N_COL = 64
DEVICES = 1024


def draw_send_count(key, part):
    key = jax.random.fold_in(key, 11)
    counts = jax.random.randint(key, (DEVICES, 3, 3), S // 4, S + 1)
    pair_ids = jnp.arange(3)
    centre = (pair_ids[:, None] == 1) & (pair_ids[None, :] == 1)
    return jnp.where(centre[None], S, counts).astype(jnp.int32)


def draw_block_start(key, part):
    key = jax.random.fold_in(key, 23)
    first_key, second_key = jax.random.split(key)
    top_row = jax.random.randint(first_key, (DEVICES, 3, 3, S), 0, OY - WIN_R + 1)
    left_col = jax.random.randint(second_key, (DEVICES, 3, 3, S), 0, OX - WIN_C + 1)
    start_cell = top_row * OX + left_col
    slot_ids = jnp.arange(S)[None, None, None, :]
    pair_ids = jnp.arange(3)
    corner_low = (pair_ids[:, None] == 0) & (pair_ids[None, :] == 0)
    corner_high = (pair_ids[:, None] == 2) & (pair_ids[None, :] == 2)
    first_slot = slot_ids == 0
    highest = (OY - WIN_R) * OX + OX - WIN_C
    start_cell = jnp.where(corner_low[None, :, :, None] & first_slot, 0, start_cell)
    start_cell = jnp.where(corner_high[None, :, :, None] & first_slot, highest, start_cell)
    return start_cell.astype(jnp.int32)


def with_ends(drawn, rng, low, top_value):
    longest = drawn.shape.index(max(drawn.shape))
    spots = []
    for shift in (0, 1):
        where = [jax.random.randint(jax.random.fold_in(rng, axis), (), 0, length) for axis, length in enumerate(drawn.shape)]
        where[longest] = (where[longest] + shift) % drawn.shape[longest]
        spots.append(tuple(where))
    return drawn.at[spots[0]].set(low).at[spots[1]].set(top_value)


def level_of(key, extent, pieces, smallest, largest):
    gain = 1.0
    for axis_at, blocks in pieces:
        steps = jax.random.uniform(jax.random.fold_in(jax.random.fold_in(key, 6), axis_at), (blocks,), jnp.float32, smallest / len(pieces), largest / len(pieces))
        gain = gain * jnp.repeat(jnp.exp(steps), extent[axis_at] // blocks).reshape((-1,) + (1,) * (len(extent) - 1 - axis_at))
    return gain


def centred(key, extent, spread, reach, shards=(), held_as=jnp.bfloat16):
    drawn = spread * jax.random.normal(key, extent, jnp.float32)
    if shards:
        drawn = drawn * level_of(key, extent, shards, -0.22, 0.18)
    return jnp.clip(drawn, -reach, reach).astype(held_as)


def setup_inputs(seed: int = 0) -> dict:
    streams_of = jax.random.split(jax.random.key(seed), 11)
    return {
        "atm_flux": centred(streams_of[0], (FIELDS, ATM_CELLS), 1.0, 6.0, ((1, 1024),), jnp.float32),
        "send_index": with_ends(jax.random.randint(streams_of[1], (DEVICES, 3, 3, S), 0, A_DEV), jax.random.fold_in(streams_of[1], 1), 0, A_DEV - 1).astype(jnp.int32),
        "send_count": draw_send_count(jax.random.fold_in(streams_of[10], 71), 0),
        "block_start": draw_block_start(jax.random.fold_in(streams_of[10], 71), 0),
        "remap_weight": jnp.clip(jnp.exp(math.log(0.03) - 2.70805 * jax.random.uniform(streams_of[4], (DEVICES, 3, 3, S, WB), jnp.float32) ** level_of(streams_of[4], (DEVICES, 3, 3, S, WB), ((0, 1024),), -0.2, 0.2)), 0.002, 0.03),
        "coupling": centred(streams_of[5], (OFIELDS, FIELDS), FIELDS ** -0.5, 1.25, (), jnp.float32),
        "ocean_state": centred(streams_of[6], (OFIELDS, NY, NX), 1.0, 6.0, ((1, 16), (2, 64)), jnp.float32),
        "velocity": jnp.clip(jax.random.uniform(streams_of[7], (2, NY, NX), jnp.float32, -0.5, 0.5) * level_of(streams_of[7], (2, NY, NX), ((1, 16), (2, 64)), -0.4, 0.0), -0.5, 0.5),
        "diffusivity": jnp.clip(jnp.exp(jax.random.uniform(streams_of[8], (OFIELDS,), jnp.float32, math.log(0.02), math.log(0.2))), 0.02, 0.2),
        "wet_mask": with_ends((jax.random.randint(streams_of[9], (NY, NX), 0, 3) < 2).astype(jnp.int32), jax.random.fold_in(streams_of[9], 1), 0, 1),
    }


PRECISE = lax.Precision.HIGHEST


def window_offsets():
    places = jnp.arange(WB, dtype=jnp.int32)
    return (places // WIN_C) * OX + places % WIN_C


def neighbour_view(field):
    leading = field.ndim - 5
    padding = [(0, 0)] * leading + [(1, 1), (1, 1), (0, 0), (0, 0), (0, 0)]
    padded = jnp.pad(field, padding)
    row_blocks = []
    for row_shift in range(3):
        col_blocks = []
        for col_shift in range(3):
            col_blocks.append(padded[..., row_shift:row_shift + N_ROW, col_shift:col_shift + N_COL, 2 - row_shift, 2 - col_shift, :])
        row_blocks.append(jnp.stack(col_blocks, axis=-2))
    return jnp.stack(row_blocks, axis=-3)


def reference(atm_flux, send_index, send_count, block_start, remap_weight, coupling, ocean_state, velocity, diffusivity, wet_mask):
    offsets = window_offsets()
    flux_dev = atm_flux.reshape(FIELDS, DEVICES, A_DEV)
    index_dev = send_index.reshape(DEVICES, 9 * S)
    picked = jnp.take_along_axis(flux_dev, index_dev[None], axis=2)
    slot_valid = (lax.broadcasted_iota(jnp.int32, (DEVICES, 3, 3, S), 3) < send_count[:, :, :, None]).astype(jnp.float32)
    slot_flux = picked.reshape(FIELDS, N_ROW, N_COL, 3, 3, S) * slot_valid.reshape(N_ROW, N_COL, 3, 3, S)[None]
    incoming = neighbour_view(slot_flux).reshape(FIELDS, DEVICES, 9 * S)
    incoming = jnp.moveaxis(incoming, 1, 0)
    live = neighbour_view(slot_valid.reshape(N_ROW, N_COL, 3, 3, S)).reshape(DEVICES, 9 * S)
    starts = block_start.reshape(DEVICES, 9 * S)
    weights = remap_weight.reshape(DEVICES, 9 * S, WB)

    def tile_forward(args):
        rec_tile, live_tile, start_tile, weight_tile = args
        cell_ids = (start_tile[:, None] + offsets[None, :]).reshape(-1)
        stacked = jnp.concatenate([rec_tile, live_tile[None]], axis=0)
        contrib = (stacked[:, :, None] * weight_tile[None]).reshape(FIELDS + 1, -1)
        totals_tile = jnp.zeros((FIELDS + 1, O_CELLS), jnp.float32).at[:, cell_ids].add(contrib)
        ocean_flux = totals_tile[:FIELDS] / jnp.maximum(totals_tile[FIELDS], 1.0)
        return jnp.dot(coupling, ocean_flux, precision=PRECISE, preferred_element_type=jnp.float32)

    forcing = lax.map(tile_forward, (incoming, live, starts, weights))
    forcing = forcing.reshape(N_ROW, N_COL, OFIELDS, OY, OX)
    forcing = jnp.transpose(forcing, (2, 0, 3, 1, 4)).reshape(OFIELDS, NY, NX)
    wet_float = wet_mask.astype(jnp.float32)
    padded = jnp.pad(ocean_state, ((0, 0), (1, 1), (1, 1)))
    east_cell = padded[:, 1:-1, 2:]
    west_cell = padded[:, 1:-1, :-2]
    north_cell = padded[:, 2:, 1:-1]
    south_cell = padded[:, :-2, 1:-1]
    laplace = east_cell + west_cell + north_cell + south_cell - 4.0 * ocean_state
    advect = 0.5 * (velocity[0] * (east_cell - west_cell) + velocity[1] * (north_cell - south_cell))
    new_state = ocean_state + wet_float * (diffusivity[:, None, None] * laplace - advect + forcing)
    surface = new_state * wet_float
    tiles = jnp.transpose(surface.reshape(OFIELDS, N_ROW, OY, N_COL, OX), (1, 3, 0, 2, 4)).reshape(DEVICES, OFIELDS, O_CELLS)

    def tile_back(args):
        surf_tile, live_tile, start_tile, weight_tile = args
        cell_ids = start_tile[:, None] + offsets[None, :]
        gathered = surf_tile[:, cell_ids]
        back_vals = jnp.einsum('ksw,sw->ks', gathered, weight_tile, precision=PRECISE)
        weight_sum = jnp.sum(weight_tile, axis=1)
        return jnp.concatenate([back_vals, weight_sum[None]], axis=0) * live_tile[None]

    back_tiles = lax.map(tile_back, (tiles, live, starts, weights))
    back_tiles = jnp.moveaxis(back_tiles, 1, 0).reshape(OFIELDS + 1, N_ROW, N_COL, 3, 3, S)
    returned = neighbour_view(back_tiles).reshape(OFIELDS + 1, -1)
    device_base = (jnp.arange(DEVICES, dtype=jnp.int32) * A_DEV)[:, None]
    global_ids = (device_base + index_dev).reshape(-1)
    gathered_all = jnp.zeros((OFIELDS + 1, ATM_CELLS), jnp.float32).at[:, global_ids].add(returned)
    atm_surface = gathered_all[:OFIELDS] / jnp.maximum(gathered_all[OFIELDS], 1.0)
    return new_state, atm_surface
```

```python
import jax
import jax.numpy as jnp
from jax import lax
from jax.experimental import pallas as pl
from jax.experimental.pallas import tpu as pltpu
from jax.sharding import PartitionSpec as P

WIN_R = 8
WIN_C = 16
OFF = 64
VMEM = pl.BlockSpec(memory_space=pltpu.VMEM)
SMEM = pl.BlockSpec(memory_space=pltpu.SMEM)
F32 = jnp.float32
BF16 = jnp.bfloat16
NT = (((1,), (1,)), ((), ()))


def lanes_of(shape):
    return lax.broadcasted_iota(jnp.int32, shape, 1)


def halves(value):
    high = value.astype(BF16)
    low = (value - high.astype(F32)).astype(BF16)
    return high, low


def pack_kernel(flux, index, count, coupling, state, parity, send1, send2, own, index_scr, flux_scr):
    slots = index.shape[2]
    even = parity[0] == 0
    index_scr[...] = jnp.zeros_like(index_scr)
    for i in range(9):
        index_scr[i : i + 1, 0:slots] = index[i]
    flux_scr[...] = jnp.zeros_like(flux_scr)
    flux_scr[:, 0 : flux.shape[1]] = lax.dot_general(
        coupling[...], flux[...], (((1,), (0,)), ((), ())),
        precision=lax.Precision.HIGHEST, preferred_element_type=F32,
    )
    mapped = flux_scr[...]
    lane = lanes_of(mapped.shape)
    groups = []
    for a in range(3):
        for b in range(3):
            used = count[a, 0, b]
            places = jnp.broadcast_to(index_scr[3 * a + b : 3 * a + b + 1, :], mapped.shape)
            picked = jnp.take_along_axis(mapped, places, axis=1)
            flag = ((lane >= OFF) & (lane < OFF + used)).astype(F32)
            groups.append(jnp.where(lane < used, picked, flag))
    rows = state.shape[0] // 8
    for b in range(3):
        up, down = groups[6 + b], groups[b]
        send1[b] = jnp.where(even, up, down)
        send2[b] = jnp.where(even, down, up)
        own[b] = groups[3 + b]
    first = state[pl.ds(0, 8, stride=rows), :]
    last = state[pl.ds(rows - 1, 8, stride=rows), :]
    send1[3] = jnp.where(even, last, first)
    send2[3] = jnp.where(even, first, last)
    west = jnp.zeros_like(mapped)
    east = jnp.zeros_like(mapped)
    width = state.shape[1]
    for y in range(rows):
        line = state[pl.ds(y, 8, stride=rows), :]
        west = jnp.where(lane == y, jnp.broadcast_to(line[:, 0:1], mapped.shape), west)
        east = jnp.where(lane == y, jnp.broadcast_to(line[:, width - 1 : width], mapped.shape), east)
    own[3] = west
    own[4] = east


def spread_kernel(start, weight, high, low, start_scr):
    slots, width = weight.shape[3], weight.shape[4]
    rows = high.shape[1] // width
    start_scr[...] = jnp.zeros_like(start_scr)
    for i in range(9):
        start_scr[i : i + 1, 0:slots] = start[i].astype(F32)
    turned = start_scr[...].T
    lane = lanes_of((slots, width))
    for p in range(3):
        for q in range(3):
            i = 3 * p + q
            first = turned[0:slots, i : i + 1].astype(jnp.int32)
            top = first // width
            left = jnp.broadcast_to(first - top * width, (slots, width))
            above = jnp.broadcast_to(top * WIN_C, (slots, width))
            across = lane - left
            inside = (across >= 0) & (across < WIN_C)
            place = jnp.where(inside, across - above, -(1 << 20))
            block = weight[0, p, q]
            for y in range(rows):
                at = place + y * WIN_C
                hit = (at >= 0) & (at < WIN_R * WIN_C)
                value = jnp.take_along_axis(block, at & (width - 1), axis=1)
                value = jnp.where(hit, value, 0.0)
                part, rest = halves(value)
                high[i * slots : (i + 1) * slots, y * width : (y + 1) * width] = part
                low[i * slots : (i + 1) * slots, y * width : (y + 1) * width] = rest


def ocean_kernel(
    row1, row2, col1, col2, own, parity, high, low, state, velocity, diffusivity, wet,
    new_state, send1, send2, back_own, surface,
):
    slots = high.shape[0] // 9
    width = state.shape[1]
    rows = state.shape[0] // 8
    even_r = parity[0] == 0
    even_c = parity[1] == 0

    def from_plus(one, two, even, i):
        return jnp.where(even, one[i], two[i])

    def from_minus(one, two, even, i):
        return jnp.where(even, two[i], one[i])

    middle = [from_minus(row1, row2, even_r, 1), own[1], from_plus(row1, row2, even_r, 1)]
    blocks = []
    for p in range(3):
        blocks += [from_minus(col1, col2, even_c, p), middle[p], from_plus(col1, col2, even_c, p)]
    south_edge = from_minus(row1, row2, even_r, 3)
    north_edge = from_plus(row1, row2, even_r, 3)
    west_edge = from_minus(col1, col2, even_c, 3)
    east_edge = from_plus(col1, col2, even_c, 3)

    fields = jnp.concatenate([block[:, 0:slots] for block in blocks], axis=1)
    flags = jnp.concatenate([block[:, OFF : OFF + slots] for block in blocks], axis=1)
    first_row = lax.broadcasted_iota(jnp.int32, flags.shape, 0) == 0
    flags = jnp.where(first_row, flags, 0.0)
    field_high = fields.astype(BF16).astype(F32)
    field_low = fields - field_high
    left_high = jnp.concatenate([field_high, flags], axis=0).astype(BF16)
    left_low = jnp.concatenate([field_low, jnp.zeros_like(flags)], axis=0).astype(BF16)
    left = jnp.concatenate([left_high, left_low], axis=0)

    lane = lanes_of((8, width))
    row_of = lax.broadcasted_iota(jnp.int32, (8, width), 0)
    one_row = jnp.where(row_of == 0, 1.0, 0.0)
    spread = jnp.zeros((8, width), F32)
    for k in range(8):
        spread = jnp.where(row_of == k, diffusivity[k], spread)
    step = 2 * width
    lines = [state[pl.ds(y, 8, stride=rows), :] for y in range(rows)]
    for part in range(rows // 2):
        cells = slice(part * step, (part + 1) * step)
        sums = jnp.dot(left, high[:, cells], preferred_element_type=F32)
        sums = sums[0:16] + sums[16:32] + jnp.dot(left_high, low[:, cells], preferred_element_type=F32)
        for y in (2 * part, 2 * part + 1):
            at = slice((y % 2) * width, (y % 2 + 1) * width)
            cover = sums[8:9, at]
            forcing = sums[0:8, at] / jnp.maximum(jnp.broadcast_to(cover, (8, width)), 1.0)
            here = lines[y]
            north = lines[y + 1] if y + 1 < rows else north_edge
            south = lines[y - 1] if y > 0 else south_edge
            east = pltpu.roll(here, width - 1, 1)
            east = jnp.where(lane == width - 1, jnp.broadcast_to(east_edge[:, y : y + 1], (8, width)), east)
            west = pltpu.roll(here, 1, 1)
            west = jnp.where(lane == 0, jnp.broadcast_to(west_edge[:, y : y + 1], (8, width)), west)
            laplace = east + west + north + south - 4.0 * here
            along = jnp.broadcast_to(velocity[0, y : y + 1, :], (8, width))
            across = jnp.broadcast_to(velocity[1, y : y + 1, :], (8, width))
            advect = 0.5 * (along * (east - west) + across * (north - south))
            mask = jnp.broadcast_to(wet[y : y + 1, :], (8, width)).astype(F32)
            fresh = here + mask * (spread * laplace - advect + forcing)
            new_state[pl.ds(y, 8, stride=rows), :] = fresh
            seen = fresh * mask
            seen_high = seen.astype(BF16).astype(F32)
            column = slice(y * width, (y + 1) * width)
            surface[0:16, column] = jnp.concatenate([seen_high, one_row], axis=0).astype(BF16)
            surface[16:32, column] = jnp.concatenate([seen - seen_high, jnp.zeros_like(seen)], axis=0).astype(BF16)
    back = lax.dot_general(surface[...], high[...], NT, preferred_element_type=F32)
    back = back[0:16] + back[16:32] + lax.dot_general(
        surface[0:16, :], low[...], NT, preferred_element_type=F32
    )
    pad = jnp.zeros((8, OFF - slots), F32)
    out = []
    for i in range(9):
        at = slice(i * slots, (i + 1) * slots)
        out.append(jnp.concatenate([back[0:8, at], pad, back[8:16, at], pad], axis=1))
    for q in range(3):
        up, down = out[6 + q], out[q]
        send1[q] = jnp.where(even_r, up, down)
        send2[q] = jnp.where(even_r, down, up)
        back_own[q] = out[3 + q]


def surface_kernel(row1, row2, col1, col2, own, parity, index, count, result, index_scr):
    slots = index.shape[2]
    cells = result.shape[1]
    even_r = parity[0] == 0
    even_c = parity[1] == 0
    index_scr[...] = jnp.zeros_like(index_scr)
    for i in range(9):
        index_scr[i : i + 1, 0:slots] = index[i]
    middle = [
        jnp.where(even_r, row2[1], row1[1]),
        own[1],
        jnp.where(even_r, row1[1], row2[1]),
    ]
    width = own.shape[2]
    lane = lanes_of((8, width))
    cell = lax.broadcasted_iota(jnp.int32, (cells, width), 0)
    total = jnp.zeros((32, cells), F32)
    for a in range(3):
        group = [
            jnp.where(even_c, col2[a], col1[a]),
            middle[a],
            jnp.where(even_c, col1[a], col2[a]),
        ]
        for b in range(3):
            used = lane < count[a, 0, b]
            block = group[b]
            value = jnp.where(used, block, 0.0)
            weights = jnp.where(used, pltpu.roll(block, OFF, 1), 0.0)
            left = jnp.concatenate([value, weights], axis=0)
            left_high = left.astype(BF16).astype(F32)
            left = jnp.concatenate([left_high, left - left_high], axis=0).astype(BF16)
            places = jnp.broadcast_to(index_scr[3 * a + b : 3 * a + b + 1, :], (cells, width))
            hot = (places == cell).astype(F32).astype(BF16)
            total = total + lax.dot_general(left, hot, NT, preferred_element_type=F32)
    total = total[0:16] + total[16:32]
    cover = jnp.maximum(jnp.broadcast_to(total[8:9], (8, cells)), 1.0)
    result[...] = total[0:8] / cover


def swaps(count):
    near = [(i, i ^ 1) for i in range(count)]
    far = [(i, i + 1) for i in range(1, count - 1, 2)]
    far = far + [(j, i) for i, j in far]
    return near, far


def exchange(send1, send2, axis):
    near, far = swaps(lax.axis_size(axis))
    two = lax.ppermute(send2, axis, far)
    one = lax.ppermute(send1, axis, near)
    return one, two


def column_sends(row1, row2, own, extra, even_r, even_c):
    minus = jnp.where(even_r, row2, row1)
    plus = jnp.where(even_r, row1, row2)
    low = jnp.stack([minus[0], own[0], plus[0]] + [edge for edge in extra[:1]])
    high = jnp.stack([minus[2], own[2], plus[2]] + [edge for edge in extra[1:]])
    return jnp.where(even_c, high, low), jnp.where(even_c, low, high)


def call(kernel, outs, scratch, specs, flops, size, *args, name):
    return pl.pallas_call(
        kernel,
        out_shape=outs,
        in_specs=specs,
        out_specs=[VMEM] * len(outs),
        scratch_shapes=scratch,
        compiler_params=pltpu.CompilerParams(vmem_limit_bytes=24 * 1024 * 1024),
        cost_estimate=pl.CostEstimate(flops=flops, bytes_accessed=size, transcendentals=0),
        name=name,
    )(*args)


def on_device(
    atm_flux,
    send_index,
    send_count,
    block_start,
    remap_weight,
    coupling,
    ocean_state,
    velocity,
    diffusivity,
    wet_mask,
):
    fields, rows, width = ocean_state.shape
    slots = send_index.shape[3]
    cells = rows * width
    parity = jnp.stack([lax.axis_index("row") % 2, lax.axis_index("col") % 2]).astype(jnp.int32)
    even_r = parity[0] == 0
    even_c = parity[1] == 0
    state = ocean_state.reshape(fields * rows, width)
    index = send_index.reshape(9, 1, slots)
    count = send_count.reshape(3, 1, 3)
    start = block_start.reshape(9, 1, slots)

    def shape(*dims, dtype=F32):
        return jax.ShapeDtypeStruct(dims, dtype)

    send1, send2, own = call(
        pack_kernel,
        [shape(4, 8, width), shape(4, 8, width), shape(5, 8, width)],
        [pltpu.VMEM((16, width), jnp.int32), pltpu.VMEM((8, width), F32)],
        [VMEM, VMEM, SMEM, VMEM, VMEM, SMEM],
        100_000, 200_000,
        atm_flux, index, count, coupling, state, parity,
        name="pack",
    )
    row1, row2 = exchange(send1, send2, "row")
    high, low = call(
        spread_kernel,
        [shape(9 * slots, cells, dtype=BF16), shape(9 * slots, cells, dtype=BF16)],
        [pltpu.VMEM((16, width), F32)],
        [VMEM, VMEM],
        20_000_000, 4_000_000,
        start, remap_weight,
        name="spread",
    )
    send1, send2 = column_sends(row1, row2, own, [own[3], own[4]], even_r, even_c)
    col1, col2 = exchange(send1, send2, "col")
    new_state, send1, send2, own = call(
        ocean_kernel,
        [shape(fields * rows, width), shape(3, 8, width), shape(3, 8, width), shape(3, 8, width)],
        [pltpu.VMEM((32, cells), BF16)],
        [VMEM] * 5 + [SMEM] + [VMEM] * 4 + [SMEM, VMEM],
        100_000_000, 4_000_000,
        row1, row2, col1, col2, own, parity, high, low, state, velocity,
        diffusivity, wet_mask,
        name="ocean",
    )
    row1, row2 = exchange(send1, send2, "row")
    send1, send2 = column_sends(row1, row2, own, [], even_r, even_c)
    col1, col2 = exchange(send1, send2, "col")
    (result,) = call(
        surface_kernel,
        [shape(fields, atm_flux.shape[1])],
        [pltpu.VMEM((16, width), jnp.int32)],
        [VMEM, VMEM, VMEM, VMEM, VMEM, SMEM, VMEM, SMEM],
        1_000_000, 200_000,
        row1, row2, col1, col2, own, parity, index, count,
        name="surface",
    )
    return new_state.reshape(ocean_state.shape), result


def solution(mesh):
    return jax.shard_map(
        on_device,
        mesh=mesh,
        in_specs=(
            P(None, ("row", "col")),
            P(("row", "col"), None, None, None),
            P(("row", "col"), None, None),
            P(("row", "col"), None, None, None),
            P(("row", "col"), None, None, None, None),
            P(),
            P(None, "row", "col"),
            P(None, "row", "col"),
            P(),
            P("row", "col"),
        ),
        out_specs=(P(None, "row", "col"), P(None, ("row", "col"))),
        check_vma=False,
    )
```

```python
import functools

import jax
import jax.numpy as jnp
from jax import lax
from jax.experimental import pallas as pl
from jax.experimental.pallas import tpu as pltpu
from jax.sharding import PartitionSpec as P

WIN_R = 8
WIN_C = 16
OFF = 64
SPLIT = 5
VMEM = pl.BlockSpec(memory_space=pltpu.VMEM)
HBM = pl.BlockSpec(memory_space=pltpu.HBM)
F32 = jnp.float32
BF16 = jnp.bfloat16
NT = (((1,), (1,)), ((), ()))


def lanes_of(shape):
    return lax.broadcasted_iota(jnp.int32, shape, 1)


def halves(value):
    high = value.astype(BF16)
    low = (value - high.astype(F32)).astype(BF16)
    return high, low


def is_even(axis):
    return lax.axis_index(axis) % 2 == 0


def pack_kernel(
    flux, index, count, coupling, state, start, weight, velocity, diffusivity, wet,
    send1, send2, own, index_kept, count_kept, state_kept, start_kept, weight_kept, velocity_kept,
    diffusivity_kept, wet_kept,
    flux_in, coupling_in, index_scr, flux_scr, sems,
):
    pairs = [
        (flux, flux_in), (coupling, coupling_in), (index, index_kept), (count, count_kept), (state, state_kept),
        (start, start_kept), (weight, weight_kept), (velocity, velocity_kept),
        (diffusivity, diffusivity_kept), (wet, wet_kept),
    ]
    copies = [pltpu.make_async_copy(source, target, sems.at[i]) for i, (source, target) in enumerate(pairs)]
    for copy in copies:
        copy.start()
    slots = index.shape[2]
    even = is_even("row")
    index_scr[...] = jnp.zeros_like(index_scr)
    flux_scr[...] = jnp.zeros_like(flux_scr)
    for copy in copies[:5]:
        copy.wait()
    for i in range(9):
        index_scr[i : i + 1, 0:slots] = index_kept[i]
    flux_scr[:, 0 : flux.shape[1]] = lax.dot_general(
        coupling_in[...], flux_in[...], (((1,), (0,)), ((), ())),
        precision=lax.Precision.HIGHEST, preferred_element_type=F32,
    )
    rows = state.shape[0] // 8
    mapped = flux_scr[...]
    lane = lanes_of(mapped.shape)
    west = jnp.zeros_like(mapped)
    east = jnp.zeros_like(mapped)
    width = state.shape[1]
    for y in range(rows):
        line = state_kept[pl.ds(y, 8, stride=rows), :]
        west = jnp.where(lane == y, jnp.broadcast_to(line[:, 0:1], mapped.shape), west)
        east = jnp.where(lane == y, jnp.broadcast_to(line[:, width - 1 : width], mapped.shape), east)
    own[3] = west
    own[4] = east
    groups = []
    for a in range(3):
        for b in range(3):
            used = jnp.broadcast_to(count_kept[a][:, b : b + 1], mapped.shape)
            places = jnp.broadcast_to(index_scr[3 * a + b : 3 * a + b + 1, :], mapped.shape)
            picked = jnp.take_along_axis(mapped, places, axis=1)
            flag = ((lane >= OFF) & (lane < OFF + used)).astype(F32)
            groups.append(jnp.where(lane < used, picked, flag))
    for b in range(3):
        up, down = groups[6 + b], groups[b]
        send1[b] = jnp.where(even, up, down)
        send2[b] = jnp.where(even, down, up)
        own[b] = groups[3 + b]
    first = state_kept[pl.ds(0, 8, stride=rows), :]
    last = state_kept[pl.ds(rows - 1, 8, stride=rows), :]
    send1[3] = jnp.where(even, last, first)
    send2[3] = jnp.where(even, first, last)
    for copy in copies[5:]:
        copy.wait()


def spread_kernel(begin, end, start, weight, after, high, low, start_scr):
    slots, width = weight.shape[3], weight.shape[4]
    rows = high.shape[1] // width
    start_scr[...] = jnp.zeros_like(start_scr)
    for i in range(begin, end):
        start_scr[i : i + 1, 0:slots] = start[i].astype(F32)
    turned = start_scr[...].T
    lane = lanes_of((slots, width))
    for i in range(begin, end):
        first = turned[0:slots, i : i + 1].astype(jnp.int32)
        top = first // width
        left = jnp.broadcast_to(first - top * width, (slots, width))
        above = jnp.broadcast_to(top * WIN_C, (slots, width))
        across = lane - left
        inside = (across >= 0) & (across < WIN_C)
        place = jnp.where(inside, across - above, -(1 << 20))
        block = weight[0, i // 3, i % 3]
        at_rows = slice((i - begin) * slots, (i - begin + 1) * slots)
        for y in range(rows):
            at = place + y * WIN_C
            hit = (at >= 0) & (at < WIN_R * WIN_C)
            value = jnp.take_along_axis(block, at & (width - 1), axis=1)
            value = jnp.where(hit, value, 0.0)
            part, rest = halves(value)
            high[at_rows, y * width : (y + 1) * width] = part
            low[at_rows, y * width : (y + 1) * width] = rest


def hot_kernel(index, count, after, hot, index_scr):
    slots = index.shape[2]
    cells, width = hot.shape[0], index_scr.shape[1]
    index_scr[...] = jnp.zeros_like(index_scr)
    for i in range(9):
        index_scr[i : i + 1, 0:slots] = index[i]
    lane = lanes_of((1, width))
    cell = lax.broadcasted_iota(jnp.int32, (cells, width), 0)
    for i in range(9):
        used = lane < jnp.broadcast_to(count[i // 3][:, i % 3 : i % 3 + 1], (1, width))
        places = jnp.where(used, index_scr[i : i + 1, :], -1)
        here = jnp.broadcast_to(places, (cells, width)) == cell
        hot[:, i * width : (i + 1) * width] = here.astype(F32).astype(BF16)


def ocean_kernel(
    row1, row2, col1, col2, own, high1, low1, high2, low2, state, velocity, diffusivity, wet,
    new_state, send1, send2, back_own, surface,
):
    split = high1.shape[0]
    slots = (split + high2.shape[0]) // 9
    width = state.shape[1]
    rows = state.shape[0] // 8
    even_r = is_even("row")
    even_c = is_even("col")

    def from_plus(one, two, even, i):
        return jnp.where(even, one[i], two[i])

    def from_minus(one, two, even, i):
        return jnp.where(even, two[i], one[i])

    middle = [from_minus(row1, row2, even_r, 1), own[1], from_plus(row1, row2, even_r, 1)]
    blocks = []
    for p in range(3):
        blocks += [from_minus(col1, col2, even_c, p), middle[p], from_plus(col1, col2, even_c, p)]
    south_edge = from_minus(row1, row2, even_r, 3)
    north_edge = from_plus(row1, row2, even_r, 3)
    west_edge = from_minus(col1, col2, even_c, 3)
    east_edge = from_plus(col1, col2, even_c, 3)

    def left_of(group):
        fields = jnp.concatenate([block[:, 0:slots] for block in group], axis=1)
        flags = jnp.concatenate([block[:, OFF : OFF + slots] for block in group], axis=1)
        first_row = lax.broadcasted_iota(jnp.int32, flags.shape, 0) == 0
        flags = jnp.where(first_row, flags, 0.0)
        field_high = fields.astype(BF16).astype(F32)
        field_low = fields - field_high
        parts = [field_high, flags, field_low, jnp.zeros_like(flags)]
        return jnp.concatenate(parts, axis=0).astype(BF16)

    left1 = left_of(blocks[: split // slots])
    left2 = left_of(blocks[split // slots :])

    lane = lanes_of((8, width))
    row_of = lax.broadcasted_iota(jnp.int32, (8, width), 0)
    one_row = jnp.where(row_of == 0, 1.0, 0.0)
    spread = jnp.zeros((8, width), F32)
    for k in range(8):
        spread = jnp.where(row_of == k, jnp.broadcast_to(diffusivity[:, k : k + 1], (8, width)), spread)
    step = 2 * width
    lines = [state[pl.ds(y, 8, stride=rows), :] for y in range(rows)]
    for part in range(rows // 2):
        cells = slice(part * step, (part + 1) * step)
        sums = jnp.dot(left1, high1[:, cells], preferred_element_type=F32)
        sums = sums + jnp.dot(left2, high2[:, cells], preferred_element_type=F32)
        rest = jnp.dot(left1[0:16], low1[:, cells], preferred_element_type=F32)
        rest = rest + jnp.dot(left2[0:16], low2[:, cells], preferred_element_type=F32)
        sums = sums[0:16] + sums[16:32] + rest
        for y in (2 * part, 2 * part + 1):
            at = slice((y % 2) * width, (y % 2 + 1) * width)
            cover = sums[8:9, at]
            forcing = sums[0:8, at] / jnp.maximum(jnp.broadcast_to(cover, (8, width)), 1.0)
            here = lines[y]
            north = lines[y + 1] if y + 1 < rows else north_edge
            south = lines[y - 1] if y > 0 else south_edge
            east = pltpu.roll(here, width - 1, 1)
            east = jnp.where(lane == width - 1, jnp.broadcast_to(east_edge[:, y : y + 1], (8, width)), east)
            west = pltpu.roll(here, 1, 1)
            west = jnp.where(lane == 0, jnp.broadcast_to(west_edge[:, y : y + 1], (8, width)), west)
            laplace = east + west + north + south - 4.0 * here
            along = jnp.broadcast_to(velocity[0, y : y + 1, :], (8, width))
            across = jnp.broadcast_to(velocity[1, y : y + 1, :], (8, width))
            advect = 0.5 * (along * (east - west) + across * (north - south))
            mask = jnp.broadcast_to(wet[y : y + 1, :], (8, width)).astype(F32)
            fresh = here + mask * (spread * laplace - advect + forcing)
            new_state[pl.ds(y, 8, stride=rows), :] = fresh
            seen = fresh * mask
            seen_high = seen.astype(BF16).astype(F32)
            column = slice(y * width, (y + 1) * width)
            surface[0:16, column] = jnp.concatenate([seen_high, one_row], axis=0).astype(BF16)
            surface[16:32, column] = jnp.concatenate([seen - seen_high, jnp.zeros_like(seen)], axis=0).astype(BF16)
    pad = jnp.zeros((8, OFF - slots), F32)
    out = []
    for high, low in ((high1, low1), (high2, low2)):
        back = lax.dot_general(surface[...], high[...], NT, preferred_element_type=F32)
        back = back[0:16] + back[16:32] + lax.dot_general(
            surface[0:16, :], low[...], NT, preferred_element_type=F32
        )
        for i in range(high.shape[0] // slots):
            at = slice(i * slots, (i + 1) * slots)
            out.append(jnp.concatenate([back[0:8, at], pad, back[8:16, at], pad], axis=1))
    for q in range(3):
        up, down = out[6 + q], out[q]
        send1[q] = jnp.where(even_r, up, down)
        send2[q] = jnp.where(even_r, down, up)
        back_own[q] = out[3 + q]


def surface_kernel(row1, row2, col1, col2, own, hot, result):
    cells = result.shape[1]
    even_r = is_even("row")
    even_c = is_even("col")
    middle = [
        jnp.where(even_r, row2[1], row1[1]),
        own[1],
        jnp.where(even_r, row1[1], row2[1]),
    ]
    blocks = []
    for a in range(3):
        blocks += [
            jnp.where(even_c, col2[a], col1[a]),
            middle[a],
            jnp.where(even_c, col1[a], col2[a]),
        ]
    values = jnp.concatenate(blocks, axis=1)
    weights = jnp.concatenate([pltpu.roll(block, OFF, 1) for block in blocks], axis=1)
    value_high = values.astype(BF16).astype(F32)
    weight_high = weights.astype(BF16).astype(F32)
    left = jnp.concatenate([value_high, weight_high, values - value_high, weights - weight_high], axis=0)
    total = lax.dot_general(left.astype(BF16), hot[...], NT, preferred_element_type=F32)
    total = total[0:16] + total[16:32]
    cover = jnp.maximum(jnp.broadcast_to(total[8:9], (8, cells)), 1.0)
    result[...] = total[0:8] / cover


def swaps(count):
    near = [(i, i ^ 1) for i in range(count)]
    far = [(i, i + 1) for i in range(1, count - 1, 2)]
    far = far + [(j, i) for i, j in far]
    return near, far


def exchange(send1, send2, axis):
    near, far = swaps(lax.axis_size(axis))
    two = lax.ppermute(send2, axis, far)
    one = lax.ppermute(send1, axis, near)
    return one, two


def column_sends(row1, row2, own, extra, even_r, even_c):
    minus = jnp.where(even_r, row2, row1)
    plus = jnp.where(even_r, row1, row2)
    low = jnp.stack([minus[0], own[0], plus[0]] + [edge for edge in extra[:1]])
    high = jnp.stack([minus[2], own[2], plus[2]] + [edge for edge in extra[1:]])
    return jnp.where(even_c, high, low), jnp.where(even_c, low, high)


def in_hbm(array):
    return pltpu.with_memory_space_constraint(array, pltpu.HBM)


def call(kernel, outs, scratch, specs, flops, size, *args, name):
    return pl.pallas_call(
        kernel,
        out_shape=outs,
        in_specs=specs,
        out_specs=[VMEM] * len(outs),
        scratch_shapes=scratch,
        compiler_params=pltpu.CompilerParams(vmem_limit_bytes=24 * 1024 * 1024),
        cost_estimate=pl.CostEstimate(flops=flops, bytes_accessed=size, transcendentals=0),
        name=name,
    )(*args)


def on_device(
    atm_flux,
    send_index,
    send_count,
    block_start,
    remap_weight,
    coupling,
    ocean_state,
    velocity,
    diffusivity,
    wet_mask,
):
    fields, rows, width = ocean_state.shape
    slots = send_index.shape[3]
    cells = rows * width
    atm_cells = atm_flux.shape[1]
    even_r = is_even("row")
    even_c = is_even("col")
    state = ocean_state.reshape(fields * rows, width)
    index = send_index.reshape(9, 1, slots)
    count = send_count.reshape(3, 1, 3)
    start = block_start.reshape(9, 1, slots)

    def shape(*dims, dtype=F32):
        return jax.ShapeDtypeStruct(dims, dtype)

    kept = [index, count, state, start, remap_weight, velocity, diffusivity.reshape(1, -1), wet_mask]
    send1, send2, own, index, count, state, start, weight, velocity, diffusivity, wet = call(
        pack_kernel,
        [shape(4, 8, width), shape(4, 8, width), shape(5, 8, width)]
        + [shape(*array.shape, dtype=array.dtype) for array in kept],
        [
            pltpu.VMEM(atm_flux.shape, F32),
            pltpu.VMEM(coupling.shape, F32),
            pltpu.VMEM((16, width), jnp.int32),
            pltpu.VMEM((8, width), F32),
            pltpu.SemaphoreType.DMA((10,)),
        ],
        [HBM] * 10,
        100_000, 1_000_000,
        *(in_hbm(array) for array in (atm_flux, index, count, coupling)),
        *(in_hbm(array) for array in kept[2:]),
        name="pack",
    )

    def spread(begin, end, after, name):
        return call(
            functools.partial(spread_kernel, begin, end),
            [shape((end - begin) * slots, cells, dtype=BF16)] * 2,
            [pltpu.VMEM((16, width), F32)],
            [VMEM, VMEM, VMEM],
            20_000_000, 4_000_000,
            start, weight, after,
            name=name,
        )

    row1, row2 = exchange(send1, send2, "row")
    high1, low1 = spread(0, SPLIT, own, "spread_one")
    row1, row2, high1, low1 = lax.optimization_barrier((row1, row2, high1, low1))
    send1, send2 = column_sends(row1, row2, own, [own[3], own[4]], even_r, even_c)
    col1, col2 = exchange(send1, send2, "col")
    high2, low2 = spread(SPLIT, 9, send1, "spread_two")
    new_state, send1, send2, own = call(
        ocean_kernel,
        [shape(fields * rows, width), shape(3, 8, width), shape(3, 8, width), shape(3, 8, width)],
        [pltpu.VMEM((32, cells), BF16)],
        [VMEM] * 13,
        100_000_000, 4_000_000,
        row1, row2, col1, col2, own, high1, low1, high2, low2, state, velocity, diffusivity, wet,
        name="ocean",
    )
    row1, row2 = exchange(send1, send2, "row")
    (hot,) = call(
        hot_kernel,
        [shape(atm_cells, 9 * width, dtype=BF16)],
        [pltpu.VMEM((16, width), jnp.int32)],
        [VMEM] * 3,
        1_000_000, 200_000,
        index, count, own,
        name="hot",
    )
    row1, row2, hot = lax.optimization_barrier((row1, row2, hot))
    send1, send2 = column_sends(row1, row2, own, [], even_r, even_c)
    col1, col2 = exchange(send1, send2, "col")
    (result,) = call(
        surface_kernel,
        [shape(fields, atm_cells)],
        [],
        [VMEM] * 6,
        1_000_000, 200_000,
        row1, row2, col1, col2, own, hot,
        name="surface",
    )
    return new_state.reshape(ocean_state.shape), result


def solution(mesh):
    return jax.shard_map(
        on_device,
        mesh=mesh,
        in_specs=(
            P(None, ("row", "col")),
            P(("row", "col"), None, None, None),
            P(("row", "col"), None, None),
            P(("row", "col"), None, None, None),
            P(("row", "col"), None, None, None, None),
            P(),
            P(None, "row", "col"),
            P(None, "row", "col"),
            P(),
            P("row", "col"),
        ),
        out_specs=(P(None, "row", "col"), P(None, ("row", "col"))),
        check_vma=False,
    )
```

```python
import functools

import jax
import jax.numpy as jnp
from jax import lax
from jax.experimental import pallas as pl
from jax.experimental.pallas import tpu as pltpu
from jax.sharding import PartitionSpec as P

WIN_R = 8
WIN_C = 16
OFF = 64
SPLIT = 4
VMEM = pl.BlockSpec(memory_space=pltpu.VMEM)
HBM = pl.BlockSpec(memory_space=pltpu.HBM)
F32 = jnp.float32
BF16 = jnp.bfloat16
NT = (((1,), (1,)), ((), ()))


def lanes_of(shape):
    return lax.broadcasted_iota(jnp.int32, shape, 1)


def halves(value):
    high = value.astype(BF16)
    low = (value - high.astype(F32)).astype(BF16)
    return high, low


def far_is_plus(axis):
    return lax.axis_index(axis) % 2 == 1


def pack_kernel(
    flux, index, count, coupling, state, start, weight, velocity, diffusivity, wet,
    send1, send2, own, index_kept, count_kept, state_kept, start_kept, weight_kept, velocity_kept,
    diffusivity_kept, wet_kept,
    flux_in, coupling_in, index_scr, flux_scr, sems,
):
    pairs = [
        (flux, flux_in), (coupling, coupling_in), (index, index_kept), (count, count_kept), (state, state_kept),
        (start, start_kept), (weight, weight_kept), (velocity, velocity_kept),
        (diffusivity, diffusivity_kept), (wet, wet_kept),
    ]
    copies = [pltpu.make_async_copy(source, target, sems.at[i]) for i, (source, target) in enumerate(pairs)]
    for copy in copies:
        copy.start()
    slots = index.shape[2]
    plus = far_is_plus("row")
    index_scr[...] = jnp.zeros_like(index_scr)
    flux_scr[...] = jnp.zeros_like(flux_scr)
    for copy in copies[:5]:
        copy.wait()
    for i in range(9):
        index_scr[i : i + 1, 0:slots] = index_kept[i]
    size = (8, flux.shape[1])
    terms = [
        jnp.broadcast_to(coupling_in[:, f : f + 1], size) * jnp.broadcast_to(flux_in[f : f + 1, :], size)
        for f in range(flux.shape[0])
    ]
    while len(terms) > 1:
        terms = [sum(terms[i : i + 2]) for i in range(0, len(terms), 2)]
    flux_scr[:, 0 : flux.shape[1]] = terms[0]
    rows = state.shape[0] // 8
    mapped = flux_scr[...]
    lane = lanes_of(mapped.shape)
    west = jnp.zeros_like(mapped)
    east = jnp.zeros_like(mapped)
    width = state.shape[1]
    for y in range(rows):
        line = state_kept[pl.ds(y, 8, stride=rows), :]
        west = jnp.where(lane == y, jnp.broadcast_to(line[:, 0:1], mapped.shape), west)
        east = jnp.where(lane == y, jnp.broadcast_to(line[:, width - 1 : width], mapped.shape), east)
    own[3] = west
    own[4] = east
    groups = []
    for a in range(3):
        for b in range(3):
            used = jnp.broadcast_to(count_kept[a][:, b : b + 1], mapped.shape)
            places = jnp.broadcast_to(index_scr[3 * a + b : 3 * a + b + 1, :], mapped.shape)
            picked = pick(mapped, places)
            flag = ((lane >= OFF) & (lane < OFF + used)).astype(F32)
            groups.append(jnp.where(lane < used, picked, flag))
    for b in range(3):
        up, down = groups[6 + b], groups[b]
        send1[b] = jnp.where(plus, up, down)
        send2[b] = jnp.where(plus, down, up)
        own[b] = groups[3 + b]
    first = state_kept[pl.ds(0, 8, stride=rows), :]
    last = state_kept[pl.ds(rows - 1, 8, stride=rows), :]
    send1[3] = jnp.where(plus, last, first)
    send2[3] = jnp.where(plus, first, last)
    for copy in copies[5:]:
        copy.wait()


def pick(table, lanes):
    return jnp.take_along_axis(table, lanes, axis=1, mode="promise_in_bounds", wrap_negative_indices=False)


def spread_kernel(begin, end, start, weight, after, high, low, start_scr):
    slots, width = weight.shape[3], weight.shape[4]
    rows = high.shape[1] // width
    start_scr[...] = jnp.zeros_like(start_scr)
    for i in range(begin, end):
        start_scr[i : i + 1, 0:slots] = start[i].astype(F32)
    turned = start_scr[...].T
    lane = lanes_of((slots, width))
    source = lax.broadcasted_iota(jnp.int32, (width, WIN_R * width), 0)
    target = lax.broadcasted_iota(jnp.int32, (width, WIN_R * width), 1)
    wanted = (target // width) * WIN_C + (target & (WIN_C - 1))
    copies = (source == wanted).astype(F32).astype(BF16)
    for i in range(begin, end):
        first = turned[0:slots, i : i + 1].astype(jnp.int32)
        top = first // width
        left = jnp.broadcast_to(first - top * width, (slots, width))
        above = jnp.broadcast_to(top * WIN_C, (slots, width))
        across = lane - left
        inside = (across >= 0) & (across < WIN_C)
        turn = (lane - left) & (WIN_C - 1)
        group = (lane - above) & (WIN_R * WIN_C - WIN_C)
        block = pick(weight[0, i // 3, i % 3], group + turn)
        top = jnp.broadcast_to(top, (slots, width))
        part = block.astype(BF16).astype(F32)
        both = jnp.concatenate([part, block - part], axis=0).astype(BF16)
        both = jnp.dot(both, copies, preferred_element_type=F32)
        at_rows = slice((i - begin) * slots, (i - begin + 1) * slots)
        for y in range(WIN_R):
            part = jnp.where(inside, both[:slots, y * width : (y + 1) * width], 0.0)
            rest = jnp.where(inside, both[slots:, y * width : (y + 1) * width], 0.0)
            late = top > y
            for to, keep in ((y, ~late), (y + WIN_R, late)):
                columns = slice(to * width, (to + 1) * width)
                high[at_rows, columns] = jnp.where(keep, part, 0.0).astype(BF16)
                low[at_rows, columns] = jnp.where(keep, rest, 0.0).astype(BF16)


def hot_kernel(index, count, fresh, hot, new_state, index_scr, sem):
    store = pltpu.make_async_copy(fresh, new_state, sem)
    store.start()
    slots = index.shape[2]
    cells, width = hot.shape[1], index_scr.shape[1]
    index_scr[...] = jnp.zeros_like(index_scr)
    for i in range(9):
        index_scr[i : i + 1, 0:slots] = index[i]
    lane = lanes_of((1, width))
    used = [lane < jnp.broadcast_to(count[i // 3][:, i % 3 : i % 3 + 1], (1, width)) for i in range(9)]
    places = [jnp.where(used[i], index_scr[i : i + 1, :], -1) for i in range(9)]
    turned = jnp.concatenate(places + [places[0]] * 7, axis=0).astype(F32).T.astype(jnp.int32)
    cell = lanes_of((width, cells))
    for i in range(9):
        here = jnp.broadcast_to(turned[:, i : i + 1], (width, cells)) == cell
        hot[i * width : (i + 1) * width, :] = here.astype(F32).astype(BF16)
    store.wait()


def ocean_kernel(
    row1, row2, col1, col2, own, high1, low1, high2, low2, state, velocity, diffusivity, wet,
    new_state, send1, send2, back_own, surface,
):
    split = high1.shape[0]
    slots = (split + high2.shape[0]) // 9
    width = state.shape[1]
    rows = state.shape[0] // 8
    plus_r = far_is_plus("row")
    plus_c = far_is_plus("col")

    def from_plus(one, two, plus, i):
        return jnp.where(plus, one[i], two[i])

    def from_minus(one, two, plus, i):
        return jnp.where(plus, two[i], one[i])

    middle = [from_minus(row1, row2, plus_r, 1), own[1], from_plus(row1, row2, plus_r, 1)]
    blocks = []
    for p in range(3):
        blocks += [from_minus(col1, col2, plus_c, p), middle[p], from_plus(col1, col2, plus_c, p)]
    south_edge = from_minus(row1, row2, plus_r, 3)
    north_edge = from_plus(row1, row2, plus_r, 3)
    west_edge = from_minus(col1, col2, plus_c, 3)
    east_edge = from_plus(col1, col2, plus_c, 3)

    def left_of(group):
        fields = jnp.concatenate([block[:, 0:slots] for block in group], axis=1)
        flags = jnp.concatenate([block[:, OFF : OFF + slots] for block in group], axis=1)
        first_row = lax.broadcasted_iota(jnp.int32, flags.shape, 0) == 0
        flags = jnp.where(first_row, flags, 0.0)
        field_high = fields.astype(BF16).astype(F32)
        field_low = fields - field_high
        parts = [field_high, flags, field_low, jnp.zeros_like(flags)]
        return jnp.concatenate(parts, axis=0).astype(BF16)

    left1 = left_of(blocks[: split // slots])
    left2 = left_of(blocks[split // slots :])

    lane = lanes_of((8, width))
    row_of = lax.broadcasted_iota(jnp.int32, (8, width), 0)
    one_row = jnp.where(row_of == 0, 1.0, 0.0)
    spread = jnp.zeros((8, width), F32)
    for k in range(8):
        spread = jnp.where(row_of == k, jnp.broadcast_to(diffusivity[:, k : k + 1], (8, width)), spread)
    step = 2 * width
    lines = [state[pl.ds(y, 8, stride=rows), :] for y in range(rows)]
    for part in range(rows // 2):
        cells = slice(part * step, (part + 1) * step)
        sums = jnp.dot(left1, high1[:, cells], preferred_element_type=F32)
        sums = sums + jnp.dot(left2, high2[:, cells], preferred_element_type=F32)
        rest = jnp.dot(left1[0:16], low1[:, cells], preferred_element_type=F32)
        rest = rest + jnp.dot(left2[0:16], low2[:, cells], preferred_element_type=F32)
        sums = sums[0:16] + sums[16:32] + rest
        for y in (2 * part, 2 * part + 1):
            at = slice((y % 2) * width, (y % 2 + 1) * width)
            cover = sums[8:9, at]
            forcing = sums[0:8, at] / jnp.maximum(jnp.broadcast_to(cover, (8, width)), 1.0)
            here = lines[y]
            north = lines[y + 1] if y + 1 < rows else north_edge
            south = lines[y - 1] if y > 0 else south_edge
            east = pltpu.roll(here, width - 1, 1)
            east = jnp.where(lane == width - 1, jnp.broadcast_to(east_edge[:, y : y + 1], (8, width)), east)
            west = pltpu.roll(here, 1, 1)
            west = jnp.where(lane == 0, jnp.broadcast_to(west_edge[:, y : y + 1], (8, width)), west)
            laplace = east + west + north + south - 4.0 * here
            along = jnp.broadcast_to(velocity[0, y : y + 1, :], (8, width))
            across = jnp.broadcast_to(velocity[1, y : y + 1, :], (8, width))
            advect = 0.5 * (along * (east - west) + across * (north - south))
            mask = jnp.broadcast_to(wet[y : y + 1, :], (8, width)).astype(F32)
            fresh = here + mask * (spread * laplace - advect + forcing)
            new_state[pl.ds(y, 8, stride=rows), :] = fresh
            seen = fresh * mask
            seen_high = seen.astype(BF16).astype(F32)
            column = slice(y * width, (y + 1) * width)
            surface[0:16, column] = jnp.concatenate([seen_high, one_row], axis=0).astype(BF16)
            surface[16:32, column] = jnp.concatenate([seen - seen_high, jnp.zeros_like(seen)], axis=0).astype(BF16)
    pad = jnp.zeros((8, OFF - slots), F32)
    out = []
    for high, low in ((high1, low1), (high2, low2)):
        back = lax.dot_general(surface[...], high[...], NT, preferred_element_type=F32)
        back = back[0:16] + back[16:32] + lax.dot_general(
            surface[0:16, :], low[...], NT, preferred_element_type=F32
        )
        for i in range(high.shape[0] // slots):
            at = slice(i * slots, (i + 1) * slots)
            out.append(jnp.concatenate([back[0:8, at], pad, back[8:16, at], pad], axis=1))
    for q in range(3):
        up, down = out[6 + q], out[q]
        send1[q] = jnp.where(plus_r, up, down)
        send2[q] = jnp.where(plus_r, down, up)
        back_own[q] = out[3 + q]


def surface_kernel(row1, row2, col1, col2, own, hot, result):
    cells = result.shape[1]
    plus_r = far_is_plus("row")
    plus_c = far_is_plus("col")
    middle = [
        jnp.where(plus_r, row2[1], row1[1]),
        own[1],
        jnp.where(plus_r, row1[1], row2[1]),
    ]
    blocks = []
    for a in range(3):
        blocks += [
            jnp.where(plus_c, col2[a], col1[a]),
            middle[a],
            jnp.where(plus_c, col1[a], col2[a]),
        ]
    values = jnp.concatenate(blocks, axis=1)
    weights = jnp.concatenate([pltpu.roll(block, OFF, 1) for block in blocks], axis=1)
    value_high = values.astype(BF16).astype(F32)
    weight_high = weights.astype(BF16).astype(F32)
    left = jnp.concatenate([value_high, weight_high, values - value_high, weights - weight_high], axis=0)
    total = jnp.dot(left.astype(BF16), hot[...], preferred_element_type=F32)
    total = total[0:16] + total[16:32]
    cover = jnp.maximum(jnp.broadcast_to(total[8:9], (8, cells)), 1.0)
    result[...] = total[0:8] / cover


def swaps(count):
    near = [(i, i ^ 1) for i in range(count)]
    far = [(i, i + 1) for i in range(1, count - 1, 2)]
    far = far + [(j, i) for i, j in far]
    return near, far


def exchange(send1, send2, axis):
    near, far = swaps(lax.axis_size(axis))
    one = lax.ppermute(send1, axis, far)
    two = lax.ppermute(send2, axis, near)
    return one, two


def column_sends(row1, row2, own, extra, plus_r, plus_c):
    minus = jnp.where(plus_r, row2, row1)
    plus = jnp.where(plus_r, row1, row2)
    low = jnp.stack([minus[0], own[0], plus[0]] + [edge for edge in extra[:1]])
    high = jnp.stack([minus[2], own[2], plus[2]] + [edge for edge in extra[1:]])
    return jnp.where(plus_c, high, low), jnp.where(plus_c, low, high)


def in_hbm(array):
    return pltpu.with_memory_space_constraint(array, pltpu.HBM)


def call(kernel, outs, scratch, specs, flops, size, *args, name, out_specs=None):
    return pl.pallas_call(
        kernel,
        out_shape=outs,
        in_specs=specs,
        out_specs=out_specs or [VMEM] * len(outs),
        scratch_shapes=scratch,
        compiler_params=pltpu.CompilerParams(vmem_limit_bytes=24 * 1024 * 1024),
        cost_estimate=pl.CostEstimate(flops=flops, bytes_accessed=size, transcendentals=0),
        name=name,
    )(*args)


def on_device(
    atm_flux,
    send_index,
    send_count,
    block_start,
    remap_weight,
    coupling,
    ocean_state,
    velocity,
    diffusivity,
    wet_mask,
):
    fields, rows, width = ocean_state.shape
    slots = send_index.shape[3]
    cells = rows * width
    atm_cells = atm_flux.shape[1]
    plus_r = far_is_plus("row")
    plus_c = far_is_plus("col")
    state = ocean_state.reshape(fields * rows, width)
    index = send_index.reshape(9, 1, slots)
    count = send_count.reshape(3, 1, 3)
    start = block_start.reshape(9, 1, slots)

    def shape(*dims, dtype=F32):
        return jax.ShapeDtypeStruct(dims, dtype)

    kept = [index, count, state, start, remap_weight, velocity, diffusivity.reshape(1, -1), wet_mask]
    send1, send2, own, index, count, state, start, weight, velocity, diffusivity, wet = call(
        pack_kernel,
        [shape(4, 8, width), shape(4, 8, width), shape(5, 8, width)]
        + [shape(*array.shape, dtype=array.dtype) for array in kept],
        [
            pltpu.VMEM(atm_flux.shape, F32),
            pltpu.VMEM(coupling.shape, F32),
            pltpu.VMEM((16, width), jnp.int32),
            pltpu.VMEM((8, width), F32),
            pltpu.SemaphoreType.DMA((10,)),
        ],
        [HBM] * 10,
        100_000, 1_000_000,
        *(in_hbm(array) for array in (atm_flux, index, count, coupling)),
        *(in_hbm(array) for array in kept[2:]),
        name="pack",
    )

    def spread(begin, end, after, name):
        return call(
            functools.partial(spread_kernel, begin, end),
            [shape((end - begin) * slots, cells, dtype=BF16)] * 2,
            [pltpu.VMEM((16, width), F32)],
            [VMEM, VMEM, VMEM],
            20_000_000, 4_000_000,
            start, weight, after,
            name=name,
        )

    row1, row2 = exchange(send1, send2, "row")
    high1, low1 = spread(0, SPLIT, own, "spread_one")
    row1, row2, high1, low1 = lax.optimization_barrier((row1, row2, high1, low1))
    send1, send2 = column_sends(row1, row2, own, [own[3], own[4]], plus_r, plus_c)
    col1, col2 = exchange(send1, send2, "col")
    high2, low2 = spread(SPLIT, 9, send1, "spread_two")
    fresh, send1, send2, own = call(
        ocean_kernel,
        [shape(fields * rows, width), shape(3, 8, width), shape(3, 8, width), shape(3, 8, width)],
        [pltpu.VMEM((32, cells), BF16)],
        [VMEM] * 13,
        100_000_000, 4_000_000,
        row1, row2, col1, col2, own, high1, low1, high2, low2, state, velocity, diffusivity, wet,
        name="ocean",
    )
    row1, row2 = exchange(send1, send2, "row")
    hot, new_state = call(
        hot_kernel,
        [shape(9 * width, atm_cells, dtype=BF16), shape(fields * rows, width)],
        [pltpu.VMEM((16, width), jnp.int32), pltpu.SemaphoreType.DMA],
        [VMEM] * 3,
        1_000_000, 200_000,
        index, count, fresh,
        out_specs=[VMEM, HBM],
        name="hot",
    )
    row1, row2, hot = lax.optimization_barrier((row1, row2, hot))
    send1, send2 = column_sends(row1, row2, own, [], plus_r, plus_c)
    col1, col2 = exchange(send1, send2, "col")
    (result,) = call(
        surface_kernel,
        [shape(fields, atm_cells)],
        [],
        [VMEM] * 6,
        1_000_000, 200_000,
        row1, row2, col1, col2, own, hot,
        name="surface",
    )
    return new_state.reshape(ocean_state.shape), result


def solution(mesh):
    return jax.shard_map(
        on_device,
        mesh=mesh,
        in_specs=(
            P(None, ("row", "col")),
            P(("row", "col"), None, None, None),
            P(("row", "col"), None, None),
            P(("row", "col"), None, None, None),
            P(("row", "col"), None, None, None, None),
            P(),
            P(None, "row", "col"),
            P(None, "row", "col"),
            P(),
            P("row", "col"),
        ),
        out_specs=(P(None, "row", "col"), P(None, ("row", "col"))),
        check_vma=False,
    )
```

```python
import functools

import jax
import jax.numpy as jnp
from jax import lax
from jax.experimental import pallas as pl
from jax.experimental.pallas import tpu as pltpu
from jax.sharding import PartitionSpec as P

WIN_R = 8
WIN_C = 16
OFF = 64
VMEM = pl.BlockSpec(memory_space=pltpu.VMEM)
HBM = pl.BlockSpec(memory_space=pltpu.HBM)
F32 = jnp.float32
BF16 = jnp.bfloat16
NT = (((1,), (1,)), ((), ()))


def lanes_of(shape):
    return lax.broadcasted_iota(jnp.int32, shape, 1)


def halves(value):
    high = value.astype(BF16)
    low = (value - high.astype(F32)).astype(BF16)
    return high, low


def far_is_plus(axis):
    return lax.axis_index(axis) % 2 == 1


def pack_kernel(
    flux, index, count, coupling, state, start, weight, velocity, diffusivity, wet,
    send1, send2, own, index_kept, count_kept, state_kept, start_kept, weight_kept, velocity_kept,
    diffusivity_kept, wet_kept,
    flux_in, coupling_in, index_scr, flux_scr, sems,
):
    pairs = [
        (flux, flux_in), (coupling, coupling_in), (index, index_kept), (count, count_kept), (state, state_kept),
        (start, start_kept), (weight, weight_kept), (velocity, velocity_kept),
        (diffusivity, diffusivity_kept), (wet, wet_kept),
    ]
    copies = [pltpu.make_async_copy(source, target, sems.at[i]) for i, (source, target) in enumerate(pairs)]
    for copy in copies:
        copy.start()
    slots = index.shape[2]
    plus = far_is_plus("row")
    index_scr[...] = jnp.zeros_like(index_scr)
    flux_scr[...] = jnp.zeros_like(flux_scr)
    for copy in copies[:5]:
        copy.wait()
    for i in range(9):
        index_scr[i : i + 1, 0:slots] = index_kept[i]
    size = (8, flux.shape[1])
    terms = [
        jnp.broadcast_to(coupling_in[:, f : f + 1], size) * jnp.broadcast_to(flux_in[f : f + 1, :], size)
        for f in range(flux.shape[0])
    ]
    while len(terms) > 1:
        terms = [sum(terms[i : i + 2]) for i in range(0, len(terms), 2)]
    flux_scr[:, 0 : flux.shape[1]] = terms[0]
    rows = state.shape[0] // 8
    mapped = flux_scr[...]
    lane = lanes_of(mapped.shape)
    west = jnp.zeros_like(mapped)
    east = jnp.zeros_like(mapped)
    width = state.shape[1]
    for y in range(rows):
        line = state_kept[pl.ds(y, 8, stride=rows), :]
        west = jnp.where(lane == y, jnp.broadcast_to(line[:, 0:1], mapped.shape), west)
        east = jnp.where(lane == y, jnp.broadcast_to(line[:, width - 1 : width], mapped.shape), east)
    own[3] = west
    own[4] = east
    groups = []
    for a in range(3):
        for b in range(3):
            used = jnp.broadcast_to(count_kept[a][:, b : b + 1], mapped.shape)
            places = jnp.broadcast_to(index_scr[3 * a + b : 3 * a + b + 1, :], mapped.shape)
            picked = pick(mapped, places)
            flag = ((lane >= OFF) & (lane < OFF + used)).astype(F32)
            groups.append(jnp.where(lane < used, picked, flag))
    for b in range(3):
        up, down = groups[6 + b], groups[b]
        send1[b] = jnp.where(plus, up, down)
        send2[b] = jnp.where(plus, down, up)
        own[b] = groups[3 + b]
    first = state_kept[pl.ds(0, 8, stride=rows), :]
    last = state_kept[pl.ds(rows - 1, 8, stride=rows), :]
    send1[3] = jnp.where(plus, last, first)
    send2[3] = jnp.where(plus, first, last)
    for copy in copies[5:]:
        copy.wait()


def pick(table, lanes):
    return jnp.take_along_axis(table, lanes, axis=1, mode="promise_in_bounds", wrap_negative_indices=False)


def spread_kernel(begin, end, start, weight, after, high, low, start_scr):
    slots, width = weight.shape[3], weight.shape[4]
    rows = high.shape[1] // width
    start_scr[...] = jnp.zeros_like(start_scr)
    for i in range(begin, end):
        start_scr[i : i + 1, 0:slots] = start[i].astype(F32)
    turned = start_scr[...].T
    lane = lanes_of((slots, width))
    source = lax.broadcasted_iota(jnp.int32, (width, WIN_R * width), 0)
    target = lax.broadcasted_iota(jnp.int32, (width, WIN_R * width), 1)
    wanted = (target // width) * WIN_C + (target & (WIN_C - 1))
    copies = (source == wanted).astype(F32).astype(BF16)
    for i in range(begin, end):
        first = turned[0:slots, i : i + 1].astype(jnp.int32)
        top = first // width
        left = jnp.broadcast_to(first - top * width, (slots, width))
        above = jnp.broadcast_to(top * WIN_C, (slots, width))
        across = lane - left
        inside = (across >= 0) & (across < WIN_C)
        turn = (lane - left) & (WIN_C - 1)
        group = (lane - above) & (WIN_R * WIN_C - WIN_C)
        block = pick(weight[0, i // 3, i % 3], group + turn)
        top = jnp.broadcast_to(top, (slots, width))
        part = block.astype(BF16).astype(F32)
        both = jnp.concatenate([part, block - part], axis=0).astype(BF16)
        both = jnp.dot(both, copies, preferred_element_type=F32)
        at_rows = slice((i - begin) * slots, (i - begin + 1) * slots)
        for y in range(WIN_R):
            part = jnp.where(inside, both[:slots, y * width : (y + 1) * width], 0.0)
            rest = jnp.where(inside, both[slots:, y * width : (y + 1) * width], 0.0)
            late = top > y
            for to, keep in ((y, ~late), (y + WIN_R, late)):
                columns = slice(to * width, (to + 1) * width)
                high[at_rows, columns] = jnp.where(keep, part, 0.0).astype(BF16)
                low[at_rows, columns] = jnp.where(keep, rest, 0.0).astype(BF16)


def hot_kernel(index, count, fresh, after, hot, new_state, index_scr, sem):
    store = pltpu.make_async_copy(fresh, new_state, sem)
    store.start()
    slots = index.shape[2]
    cells, width = hot.shape[1], index_scr.shape[1]
    index_scr[...] = jnp.zeros_like(index_scr)
    for i in range(9):
        index_scr[i : i + 1, 0:slots] = index[i]
    lane = lanes_of((1, width))
    used = [lane < jnp.broadcast_to(count[i // 3][:, i % 3 : i % 3 + 1], (1, width)) for i in range(9)]
    places = [jnp.where(used[i], index_scr[i : i + 1, :], -1) for i in range(9)]
    turned = jnp.concatenate(places + [places[0]] * 7, axis=0).astype(F32).T.astype(jnp.int32)
    cell = lanes_of((width, cells))
    for i in range(9):
        here = jnp.broadcast_to(turned[:, i : i + 1], (width, cells)) == cell
        hot[i * width : (i + 1) * width, :] = here.astype(F32).astype(BF16)
    store.wait()


def ocean_kernel(
    row1, row2, col1, col2, own, high, low, state, velocity, diffusivity, wet,
    new_state, send1, send2, back_own, surface,
):
    slots = high.shape[0] // 9
    width = state.shape[1]
    rows = state.shape[0] // 8
    plus_r = far_is_plus("row")
    plus_c = far_is_plus("col")

    def from_plus(one, two, plus, i):
        return jnp.where(plus, one[i], two[i])

    def from_minus(one, two, plus, i):
        return jnp.where(plus, two[i], one[i])

    middle = [from_minus(row1, row2, plus_r, 1), own[1], from_plus(row1, row2, plus_r, 1)]
    blocks = []
    for p in range(3):
        blocks += [from_minus(col1, col2, plus_c, p), middle[p], from_plus(col1, col2, plus_c, p)]
    south_edge = from_minus(row1, row2, plus_r, 3)
    north_edge = from_plus(row1, row2, plus_r, 3)
    west_edge = from_minus(col1, col2, plus_c, 3)
    east_edge = from_plus(col1, col2, plus_c, 3)

    def left_of(group):
        fields = jnp.concatenate([block[:, 0:slots] for block in group], axis=1)
        flags = jnp.concatenate([block[:, OFF : OFF + slots] for block in group], axis=1)
        first_row = lax.broadcasted_iota(jnp.int32, flags.shape, 0) == 0
        flags = jnp.where(first_row, flags, 0.0)
        field_high = fields.astype(BF16).astype(F32)
        field_low = fields - field_high
        parts = [field_high, flags, field_low, jnp.zeros_like(flags)]
        return jnp.concatenate(parts, axis=0).astype(BF16)

    left = left_of(blocks)

    lane = lanes_of((8, width))
    row_of = lax.broadcasted_iota(jnp.int32, (8, width), 0)
    one_row = jnp.where(row_of == 0, 1.0, 0.0)
    spread = jnp.zeros((8, width), F32)
    for k in range(8):
        spread = jnp.where(row_of == k, jnp.broadcast_to(diffusivity[:, k : k + 1], (8, width)), spread)
    step = 2 * width
    lines = [state[pl.ds(y, 8, stride=rows), :] for y in range(rows)]
    for part in range(rows // 2):
        cells = slice(part * step, (part + 1) * step)
        sums = jnp.dot(left, high[:, cells], preferred_element_type=F32)
        rest = jnp.dot(left[0:16], low[:, cells], preferred_element_type=F32)
        sums = sums[0:16] + sums[16:32] + rest
        for y in (2 * part, 2 * part + 1):
            at = slice((y % 2) * width, (y % 2 + 1) * width)
            cover = sums[8:9, at]
            forcing = sums[0:8, at] / jnp.maximum(jnp.broadcast_to(cover, (8, width)), 1.0)
            here = lines[y]
            north = lines[y + 1] if y + 1 < rows else north_edge
            south = lines[y - 1] if y > 0 else south_edge
            east = pltpu.roll(here, width - 1, 1)
            east = jnp.where(lane == width - 1, jnp.broadcast_to(east_edge[:, y : y + 1], (8, width)), east)
            west = pltpu.roll(here, 1, 1)
            west = jnp.where(lane == 0, jnp.broadcast_to(west_edge[:, y : y + 1], (8, width)), west)
            laplace = east + west + north + south - 4.0 * here
            along = jnp.broadcast_to(velocity[0, y : y + 1, :], (8, width))
            across = jnp.broadcast_to(velocity[1, y : y + 1, :], (8, width))
            advect = 0.5 * (along * (east - west) + across * (north - south))
            mask = jnp.broadcast_to(wet[y : y + 1, :], (8, width)).astype(F32)
            fresh = here + mask * (spread * laplace - advect + forcing)
            new_state[pl.ds(y, 8, stride=rows), :] = fresh
            seen = fresh * mask
            seen_high = seen.astype(BF16).astype(F32)
            column = slice(y * width, (y + 1) * width)
            surface[0:16, column] = jnp.concatenate([seen_high, one_row], axis=0).astype(BF16)
            surface[16:32, column] = jnp.concatenate([seen - seen_high, jnp.zeros_like(seen)], axis=0).astype(BF16)
    pad = jnp.zeros((8, OFF - slots), F32)
    out = []
    back = lax.dot_general(surface[...], high[...], NT, preferred_element_type=F32)
    back = back[0:16] + back[16:32] + lax.dot_general(
        surface[0:16, :], low[...], NT, preferred_element_type=F32
    )
    for i in range(9):
        at = slice(i * slots, (i + 1) * slots)
        out.append(jnp.concatenate([back[0:8, at], pad, back[8:16, at], pad], axis=1))
    for q in range(3):
        up, down = out[6 + q], out[q]
        send1[q] = jnp.where(plus_r, up, down)
        send2[q] = jnp.where(plus_r, down, up)
        back_own[q] = out[3 + q]


def surface_kernel(row1, row2, col1, col2, own, hot, result):
    cells = result.shape[1]
    plus_r = far_is_plus("row")
    plus_c = far_is_plus("col")
    middle = [
        jnp.where(plus_r, row2[1], row1[1]),
        own[1],
        jnp.where(plus_r, row1[1], row2[1]),
    ]
    blocks = []
    for a in range(3):
        blocks += [
            jnp.where(plus_c, col2[a], col1[a]),
            middle[a],
            jnp.where(plus_c, col1[a], col2[a]),
        ]
    values = jnp.concatenate(blocks, axis=1)
    weights = jnp.concatenate([pltpu.roll(block, OFF, 1) for block in blocks], axis=1)
    value_high = values.astype(BF16).astype(F32)
    weight_high = weights.astype(BF16).astype(F32)
    left = jnp.concatenate([value_high, weight_high, values - value_high, weights - weight_high], axis=0)
    total = jnp.dot(left.astype(BF16), hot[...], preferred_element_type=F32)
    total = total[0:16] + total[16:32]
    cover = jnp.maximum(jnp.broadcast_to(total[8:9], (8, cells)), 1.0)
    result[...] = total[0:8] / cover


def swaps(count):
    near = [(i, i ^ 1) for i in range(count)]
    far = [(i, i + 1) for i in range(1, count - 1, 2)]
    far = far + [(j, i) for i, j in far]
    return near, far


def exchange(send1, send2, axis):
    near, far = swaps(lax.axis_size(axis))
    one = lax.ppermute(send1, axis, far)
    send2, _ = lax.optimization_barrier((send2, send1))
    two = lax.ppermute(send2, axis, near)
    return one, two


def column_sends(row1, row2, own, extra, plus_r, plus_c):
    minus = jnp.where(plus_r, row2, row1)
    plus = jnp.where(plus_r, row1, row2)
    low = jnp.stack([minus[0], own[0], plus[0]] + [edge for edge in extra[:1]])
    high = jnp.stack([minus[2], own[2], plus[2]] + [edge for edge in extra[1:]])
    return jnp.where(plus_c, high, low), jnp.where(plus_c, low, high)


def in_hbm(array):
    return pltpu.with_memory_space_constraint(array, pltpu.HBM)


def call(kernel, outs, scratch, specs, flops, size, *args, name, out_specs=None):
    return pl.pallas_call(
        kernel,
        out_shape=outs,
        in_specs=specs,
        out_specs=out_specs or [VMEM] * len(outs),
        scratch_shapes=scratch,
        compiler_params=pltpu.CompilerParams(vmem_limit_bytes=24 * 1024 * 1024),
        cost_estimate=pl.CostEstimate(flops=flops, bytes_accessed=size, transcendentals=0),
        name=name,
    )(*args)


def on_device(
    atm_flux,
    send_index,
    send_count,
    block_start,
    remap_weight,
    coupling,
    ocean_state,
    velocity,
    diffusivity,
    wet_mask,
):
    fields, rows, width = ocean_state.shape
    slots = send_index.shape[3]
    cells = rows * width
    atm_cells = atm_flux.shape[1]
    plus_r = far_is_plus("row")
    plus_c = far_is_plus("col")
    state = ocean_state.reshape(fields * rows, width)
    index = send_index.reshape(9, 1, slots)
    count = send_count.reshape(3, 1, 3)
    start = block_start.reshape(9, 1, slots)

    def shape(*dims, dtype=F32):
        return jax.ShapeDtypeStruct(dims, dtype)

    kept = [index, count, state, start, remap_weight, velocity, diffusivity.reshape(1, -1), wet_mask]
    send1, send2, own, index, count, state, start, weight, velocity, diffusivity, wet = call(
        pack_kernel,
        [shape(4, 8, width), shape(4, 8, width), shape(5, 8, width)]
        + [shape(*array.shape, dtype=array.dtype) for array in kept],
        [
            pltpu.VMEM(atm_flux.shape, F32),
            pltpu.VMEM(coupling.shape, F32),
            pltpu.VMEM((16, width), jnp.int32),
            pltpu.VMEM((8, width), F32),
            pltpu.SemaphoreType.DMA((10,)),
        ],
        [HBM] * 10,
        100_000, 1_000_000,
        *(in_hbm(array) for array in (atm_flux, index, count, coupling)),
        *(in_hbm(array) for array in kept[2:]),
        name="pack",
    )

    def spread(after):
        return call(
            functools.partial(spread_kernel, 0, 9),
            [shape(9 * slots, cells, dtype=BF16)] * 2,
            [pltpu.VMEM((16, width), F32)],
            [VMEM, VMEM, VMEM],
            20_000_000, 4_000_000,
            start, weight, after,
            name="spread",
        )

    row1, row2 = exchange(send1, send2, "row")
    send1, send2 = column_sends(row1, row2, own, [own[3], own[4]], plus_r, plus_c)
    col1, col2 = exchange(send1, send2, "col")
    high, low = spread(send1)
    fresh, send1, send2, own = call(
        ocean_kernel,
        [shape(fields * rows, width), shape(3, 8, width), shape(3, 8, width), shape(3, 8, width)],
        [pltpu.VMEM((32, cells), BF16)],
        [VMEM] * 11,
        100_000_000, 4_000_000,
        row1, row2, col1, col2, own, high, low, state, velocity, diffusivity, wet,
        name="ocean",
    )
    row1, row2 = exchange(send1, send2, "row")
    send1, send2 = column_sends(row1, row2, own, [], plus_r, plus_c)
    col1, col2 = exchange(send1, send2, "col")
    hot, new_state = call(
        hot_kernel,
        [shape(9 * width, atm_cells, dtype=BF16), shape(fields * rows, width)],
        [pltpu.VMEM((16, width), jnp.int32), pltpu.SemaphoreType.DMA],
        [VMEM] * 4,
        1_000_000, 200_000,
        index, count, fresh, send1,
        out_specs=[VMEM, HBM],
        name="hot",
    )
    (result,) = call(
        surface_kernel,
        [shape(fields, atm_cells)],
        [],
        [VMEM] * 6,
        1_000_000, 200_000,
        row1, row2, col1, col2, own, hot,
        name="surface",
    )
    return new_state.reshape(ocean_state.shape), result


def solution(mesh):
    return jax.shard_map(
        on_device,
        mesh=mesh,
        in_specs=(
            P(None, ("row", "col")),
            P(("row", "col"), None, None, None),
            P(("row", "col"), None, None),
            P(("row", "col"), None, None, None),
            P(("row", "col"), None, None, None, None),
            P(),
            P(None, "row", "col"),
            P(None, "row", "col"),
            P(),
            P("row", "col"),
        ),
        out_specs=(P(None, "row", "col"), P(None, ("row", "col"))),
        check_vma=False,
    )
```

```python
import functools

import jax
import jax.numpy as jnp
from jax import lax
from jax.experimental import pallas as pl
from jax.experimental.pallas import tpu as pltpu
from jax.sharding import PartitionSpec as P

WIN_R = 8
WIN_C = 16
OFF = 64
VMEM = pl.BlockSpec(memory_space=pltpu.VMEM)
HBM = pl.BlockSpec(memory_space=pltpu.HBM)
F32 = jnp.float32
BF16 = jnp.bfloat16
NT = (((1,), (1,)), ((), ()))


def lanes_of(shape):
    return lax.broadcasted_iota(jnp.int32, shape, 1)


def halves(value):
    high = value.astype(BF16)
    low = (value - high.astype(F32)).astype(BF16)
    return high, low


def far_is_plus(axis):
    return lax.axis_index(axis) % 2 == 1


def pack_kernel(
    flux, index, count, coupling, state, start, weight, velocity, diffusivity, wet,
    send1, send2, own, index_kept, count_kept, state_kept, start_kept, weight_kept, velocity_kept,
    diffusivity_kept, wet_kept,
    flux_in, coupling_in, index_scr, flux_scr, sems,
):
    pairs = [
        (flux, flux_in), (coupling, coupling_in), (index, index_kept), (count, count_kept), (state, state_kept),
        (start, start_kept), (weight, weight_kept), (velocity, velocity_kept),
        (diffusivity, diffusivity_kept), (wet, wet_kept),
    ]
    copies = [pltpu.make_async_copy(source, target, sems.at[i]) for i, (source, target) in enumerate(pairs)]
    for copy in copies:
        copy.start()
    slots = index.shape[2]
    plus = far_is_plus("row")
    index_scr[...] = jnp.zeros_like(index_scr)
    flux_scr[...] = jnp.zeros_like(flux_scr)
    for copy in copies[:5]:
        copy.wait()
    for i in range(9):
        index_scr[i : i + 1, 0:slots] = index_kept[i]
    size = (8, flux.shape[1])
    terms = [
        jnp.broadcast_to(coupling_in[:, f : f + 1], size) * jnp.broadcast_to(flux_in[f : f + 1, :], size)
        for f in range(flux.shape[0])
    ]
    while len(terms) > 1:
        terms = [sum(terms[i : i + 2]) for i in range(0, len(terms), 2)]
    flux_scr[:, 0 : flux.shape[1]] = terms[0]
    rows = state.shape[0] // 8
    mapped = flux_scr[...]
    lane = lanes_of(mapped.shape)
    west = jnp.zeros_like(mapped)
    east = jnp.zeros_like(mapped)
    width = state.shape[1]
    for y in range(rows):
        line = state_kept[pl.ds(y, 8, stride=rows), :]
        west = jnp.where(lane == y, jnp.broadcast_to(line[:, 0:1], mapped.shape), west)
        east = jnp.where(lane == y, jnp.broadcast_to(line[:, width - 1 : width], mapped.shape), east)
    own[3] = west
    own[4] = east
    groups = []
    for a in range(3):
        for b in range(3):
            used = jnp.broadcast_to(count_kept[a][:, b : b + 1], mapped.shape)
            places = jnp.broadcast_to(index_scr[3 * a + b : 3 * a + b + 1, :], mapped.shape)
            picked = pick(mapped, places)
            flag = ((lane >= OFF) & (lane < OFF + used)).astype(F32)
            groups.append(jnp.where(lane < used, picked, flag))
    for b in range(3):
        up, down = groups[6 + b], groups[b]
        send1[b] = jnp.where(plus, up, down)
        send2[b] = jnp.where(plus, down, up)
        own[b] = groups[3 + b]
    first = state_kept[pl.ds(0, 8, stride=rows), :]
    last = state_kept[pl.ds(rows - 1, 8, stride=rows), :]
    send1[3] = jnp.where(plus, last, first)
    send2[3] = jnp.where(plus, first, last)
    for copy in copies[5:]:
        copy.wait()


def pick(table, lanes):
    return jnp.take_along_axis(table, lanes, axis=1, mode="promise_in_bounds", wrap_negative_indices=False)


def spread_kernel(begin, end, start, weight, after, high, low, start_scr):
    slots, width = weight.shape[3], weight.shape[4]
    rows = high.shape[1] // width
    start_scr[...] = jnp.zeros_like(start_scr)
    for i in range(begin, end):
        start_scr[i : i + 1, 0:slots] = start[i].astype(F32)
    turned = start_scr[...].T
    lane = lanes_of((slots, width))
    source = lax.broadcasted_iota(jnp.int32, (width, WIN_R * width), 0)
    target = lax.broadcasted_iota(jnp.int32, (width, WIN_R * width), 1)
    wanted = (target // width) * WIN_C + (target & (WIN_C - 1))
    copies = (source == wanted).astype(F32).astype(BF16)
    for i in range(begin, end):
        first = turned[0:slots, i : i + 1].astype(jnp.int32)
        top = first // width
        left = jnp.broadcast_to(first - top * width, (slots, width))
        above = jnp.broadcast_to(top * WIN_C, (slots, width))
        across = lane - left
        inside = (across >= 0) & (across < WIN_C)
        turn = (lane - left) & (WIN_C - 1)
        group = (lane - above) & (WIN_R * WIN_C - WIN_C)
        block = pick(weight[0, i // 3, i % 3], group + turn)
        top = jnp.broadcast_to(top, (slots, width))
        part = block.astype(BF16).astype(F32)
        both = jnp.concatenate([part, block - part], axis=0).astype(BF16)
        both = jnp.dot(both, copies, preferred_element_type=F32)
        at_rows = slice((i - begin) * slots, (i - begin + 1) * slots)
        for y in range(WIN_R):
            part = jnp.where(inside, both[:slots, y * width : (y + 1) * width], 0.0)
            rest = jnp.where(inside, both[slots:, y * width : (y + 1) * width], 0.0)
            late = top > y
            for to, keep in ((y, ~late), (y + WIN_R, late)):
                columns = slice(to * width, (to + 1) * width)
                high[at_rows, columns] = jnp.where(keep, part, 0.0).astype(BF16)
                low[at_rows, columns] = jnp.where(keep, rest, 0.0).astype(BF16)


def hot_kernel(index, count, fresh, hot, new_state, index_scr, sem):
    store = pltpu.make_async_copy(fresh, new_state, sem)
    store.start()
    slots = index.shape[2]
    cells, width = hot.shape[1], index_scr.shape[1]
    index_scr[...] = jnp.zeros_like(index_scr)
    for i in range(9):
        index_scr[i : i + 1, 0:slots] = index[i]
    lane = lanes_of((1, width))
    used = [lane < jnp.broadcast_to(count[i // 3][:, i % 3 : i % 3 + 1], (1, width)) for i in range(9)]
    places = [jnp.where(used[i], index_scr[i : i + 1, :], -1) for i in range(9)]
    turned = jnp.concatenate(places + [places[0]] * 7, axis=0).astype(F32).T.astype(jnp.int32)
    cell = lanes_of((width, cells))
    for i in range(9):
        here = jnp.broadcast_to(turned[:, i : i + 1], (width, cells)) == cell
        hot[i * width : (i + 1) * width, :] = here.astype(F32).astype(BF16)
    store.wait()


def ocean_kernel(
    row1, row2, col1, col2, own, high, low, state, velocity, diffusivity, wet,
    new_state, send1, send2, back_own, surface,
):
    slots = high.shape[0] // 9
    width = state.shape[1]
    rows = state.shape[0] // 8
    plus_r = far_is_plus("row")
    plus_c = far_is_plus("col")

    def from_plus(one, two, plus, i):
        return jnp.where(plus, one[i], two[i])

    def from_minus(one, two, plus, i):
        return jnp.where(plus, two[i], one[i])

    middle = [from_minus(row1, row2, plus_r, 1), own[1], from_plus(row1, row2, plus_r, 1)]
    blocks = []
    for p in range(3):
        blocks += [from_minus(col1, col2, plus_c, p), middle[p], from_plus(col1, col2, plus_c, p)]
    south_edge = from_minus(row1, row2, plus_r, 3)
    north_edge = from_plus(row1, row2, plus_r, 3)
    west_edge = from_minus(col1, col2, plus_c, 3)
    east_edge = from_plus(col1, col2, plus_c, 3)

    def left_of(group):
        fields = jnp.concatenate([block[:, 0:slots] for block in group], axis=1)
        flags = jnp.concatenate([block[:, OFF : OFF + slots] for block in group], axis=1)
        first_row = lax.broadcasted_iota(jnp.int32, flags.shape, 0) == 0
        flags = jnp.where(first_row, flags, 0.0)
        field_high = fields.astype(BF16).astype(F32)
        field_low = fields - field_high
        parts = [field_high, flags, field_low, jnp.zeros_like(flags)]
        return jnp.concatenate(parts, axis=0).astype(BF16)

    left = left_of(blocks)

    lane = lanes_of((8, width))
    row_of = lax.broadcasted_iota(jnp.int32, (8, width), 0)
    one_row = jnp.where(row_of == 0, 1.0, 0.0)
    spread = jnp.zeros((8, width), F32)
    for k in range(8):
        spread = jnp.where(row_of == k, jnp.broadcast_to(diffusivity[:, k : k + 1], (8, width)), spread)
    step = 2 * width
    lines = [state[pl.ds(y, 8, stride=rows), :] for y in range(rows)]
    for part in range(rows // 2):
        cells = slice(part * step, (part + 1) * step)
        sums = jnp.dot(left, high[:, cells], preferred_element_type=F32)
        rest = jnp.dot(left[0:16], low[:, cells], preferred_element_type=F32)
        sums = sums[0:16] + sums[16:32] + rest
        for y in (2 * part, 2 * part + 1):
            at = slice((y % 2) * width, (y % 2 + 1) * width)
            cover = sums[8:9, at]
            forcing = sums[0:8, at] / jnp.maximum(jnp.broadcast_to(cover, (8, width)), 1.0)
            here = lines[y]
            north = lines[y + 1] if y + 1 < rows else north_edge
            south = lines[y - 1] if y > 0 else south_edge
            east = pltpu.roll(here, width - 1, 1)
            east = jnp.where(lane == width - 1, jnp.broadcast_to(east_edge[:, y : y + 1], (8, width)), east)
            west = pltpu.roll(here, 1, 1)
            west = jnp.where(lane == 0, jnp.broadcast_to(west_edge[:, y : y + 1], (8, width)), west)
            laplace = east + west + north + south - 4.0 * here
            along = jnp.broadcast_to(velocity[0, y : y + 1, :], (8, width))
            across = jnp.broadcast_to(velocity[1, y : y + 1, :], (8, width))
            advect = 0.5 * (along * (east - west) + across * (north - south))
            mask = jnp.broadcast_to(wet[y : y + 1, :], (8, width)).astype(F32)
            fresh = here + mask * (spread * laplace - advect + forcing)
            new_state[pl.ds(y, 8, stride=rows), :] = fresh
            seen = fresh * mask
            seen_high = seen.astype(BF16).astype(F32)
            column = slice(y * width, (y + 1) * width)
            surface[0:16, column] = jnp.concatenate([seen_high, one_row], axis=0).astype(BF16)
            surface[16:32, column] = jnp.concatenate([seen - seen_high, jnp.zeros_like(seen)], axis=0).astype(BF16)
    pad = jnp.zeros((8, OFF - slots), F32)
    out = []
    back = lax.dot_general(surface[...], high[...], NT, preferred_element_type=F32)
    back = back[0:16] + back[16:32] + lax.dot_general(
        surface[0:16, :], low[...], NT, preferred_element_type=F32
    )
    for i in range(9):
        at = slice(i * slots, (i + 1) * slots)
        out.append(jnp.concatenate([back[0:8, at], pad, back[8:16, at], pad], axis=1))
    for p in range(3):
        up, down = out[3 * p + 2], out[3 * p]
        send1[p] = jnp.where(plus_c, up, down)
        send2[p] = jnp.where(plus_c, down, up)
        back_own[p] = out[3 * p + 1]


def surface_kernel(row1, row2, col1, col2, own, hot, result):
    cells = result.shape[1]
    plus_r = far_is_plus("row")
    plus_c = far_is_plus("col")
    middle = [
        jnp.where(plus_c, col2[1], col1[1]),
        own[1],
        jnp.where(plus_c, col1[1], col2[1]),
    ]
    blocks = [jnp.where(plus_r, row2[b], row1[b]) for b in range(3)]
    blocks += middle
    blocks += [jnp.where(plus_r, row1[b], row2[b]) for b in range(3)]
    values = jnp.concatenate(blocks, axis=1)
    weights = jnp.concatenate([pltpu.roll(block, OFF, 1) for block in blocks], axis=1)
    value_high = values.astype(BF16).astype(F32)
    weight_high = weights.astype(BF16).astype(F32)
    left = jnp.concatenate([value_high, weight_high, values - value_high, weights - weight_high], axis=0)
    total = jnp.dot(left.astype(BF16), hot[...], preferred_element_type=F32)
    total = total[0:16] + total[16:32]
    cover = jnp.maximum(jnp.broadcast_to(total[8:9], (8, cells)), 1.0)
    result[...] = total[0:8] / cover


def swaps(count):
    near = [(i, i ^ 1) for i in range(count)]
    far = [(i, i + 1) for i in range(1, count - 1, 2)]
    far = far + [(j, i) for i, j in far]
    return near, far


def exchange(send1, send2, axis):
    near, far = swaps(lax.axis_size(axis))
    one = lax.ppermute(send1, axis, far)
    send2, _ = lax.optimization_barrier((send2, send1))
    two = lax.ppermute(send2, axis, near)
    return one, two


def forward_sends(one, two, own, extra, plus_before, plus_next):
    minus = jnp.where(plus_before, two, one)
    plus = jnp.where(plus_before, one, two)
    low = jnp.stack([minus[0], own[0], plus[0]] + extra[:1])
    high = jnp.stack([minus[2], own[2], plus[2]] + extra[1:])
    return jnp.where(plus_next, high, low), jnp.where(plus_next, low, high)


def in_hbm(array):
    return pltpu.with_memory_space_constraint(array, pltpu.HBM)


def call(kernel, outs, scratch, specs, flops, size, *args, name, out_specs=None):
    return pl.pallas_call(
        kernel,
        out_shape=outs,
        in_specs=specs,
        out_specs=out_specs or [VMEM] * len(outs),
        scratch_shapes=scratch,
        compiler_params=pltpu.CompilerParams(vmem_limit_bytes=24 * 1024 * 1024),
        cost_estimate=pl.CostEstimate(flops=flops, bytes_accessed=size, transcendentals=0),
        name=name,
    )(*args)


def on_device(
    atm_flux,
    send_index,
    send_count,
    block_start,
    remap_weight,
    coupling,
    ocean_state,
    velocity,
    diffusivity,
    wet_mask,
):
    fields, rows, width = ocean_state.shape
    slots = send_index.shape[3]
    cells = rows * width
    atm_cells = atm_flux.shape[1]
    plus_r = far_is_plus("row")
    plus_c = far_is_plus("col")
    state = ocean_state.reshape(fields * rows, width)
    index = send_index.reshape(9, 1, slots)
    count = send_count.reshape(3, 1, 3)
    start = block_start.reshape(9, 1, slots)

    def shape(*dims, dtype=F32):
        return jax.ShapeDtypeStruct(dims, dtype)

    kept = [index, count, state, start, remap_weight, velocity, diffusivity.reshape(1, -1), wet_mask]
    send1, send2, own, index, count, state, start, weight, velocity, diffusivity, wet = call(
        pack_kernel,
        [shape(4, 8, width), shape(4, 8, width), shape(5, 8, width)]
        + [shape(*array.shape, dtype=array.dtype) for array in kept],
        [
            pltpu.VMEM(atm_flux.shape, F32),
            pltpu.VMEM(coupling.shape, F32),
            pltpu.VMEM((16, width), jnp.int32),
            pltpu.VMEM((8, width), F32),
            pltpu.SemaphoreType.DMA((10,)),
        ],
        [HBM] * 10,
        100_000, 1_000_000,
        *(in_hbm(array) for array in (atm_flux, index, count, coupling)),
        *(in_hbm(array) for array in kept[2:]),
        name="pack",
    )

    def spread(after):
        return call(
            functools.partial(spread_kernel, 0, 9),
            [shape(9 * slots, cells, dtype=BF16)] * 2,
            [pltpu.VMEM((16, width), F32)],
            [VMEM, VMEM, VMEM],
            20_000_000, 4_000_000,
            start, weight, after,
            name="spread",
        )

    row1, row2 = exchange(send1, send2, "row")
    send1, send2 = forward_sends(row1, row2, own, [own[3], own[4]], plus_r, plus_c)
    col1, col2 = exchange(send1, send2, "col")
    high, low = spread(send1)
    fresh, send1, send2, own = call(
        ocean_kernel,
        [shape(fields * rows, width), shape(3, 8, width), shape(3, 8, width), shape(3, 8, width)],
        [pltpu.VMEM((32, cells), BF16)],
        [VMEM] * 11,
        100_000_000, 4_000_000,
        row1, row2, col1, col2, own, high, low, state, velocity, diffusivity, wet,
        name="ocean",
    )
    col1, col2 = exchange(send1, send2, "col")
    hot, new_state = call(
        hot_kernel,
        [shape(9 * width, atm_cells, dtype=BF16), shape(fields * rows, width)],
        [pltpu.VMEM((16, width), jnp.int32), pltpu.SemaphoreType.DMA],
        [VMEM] * 3,
        1_000_000, 200_000,
        index, count, fresh,
        out_specs=[VMEM, HBM],
        name="hot",
    )
    col1, col2, hot = lax.optimization_barrier((col1, col2, hot))
    send1, send2 = forward_sends(col1, col2, own, [], plus_c, plus_r)
    row1, row2 = exchange(send1, send2, "row")
    (result,) = call(
        surface_kernel,
        [shape(fields, atm_cells)],
        [],
        [VMEM] * 6,
        1_000_000, 200_000,
        row1, row2, col1, col2, own, hot,
        name="surface",
    )
    return new_state.reshape(ocean_state.shape), result


def solution(mesh):
    return jax.shard_map(
        on_device,
        mesh=mesh,
        in_specs=(
            P(None, ("row", "col")),
            P(("row", "col"), None, None, None),
            P(("row", "col"), None, None),
            P(("row", "col"), None, None, None),
            P(("row", "col"), None, None, None, None),
            P(),
            P(None, "row", "col"),
            P(None, "row", "col"),
            P(),
            P("row", "col"),
        ),
        out_specs=(P(None, "row", "col"), P(None, ("row", "col"))),
        check_vma=False,
    )
```

```python
import jax
import jax.numpy as jnp
from jax import lax
from jax.experimental import pallas as pl
from jax.experimental.pallas import tpu as pltpu
from jax.sharding import PartitionSpec as P

WIN_R = 8
WIN_C = 16
OFF = 64
VMEM = pl.BlockSpec(memory_space=pltpu.VMEM)
HBM = pl.BlockSpec(memory_space=pltpu.HBM)
F32 = jnp.float32
BF16 = jnp.bfloat16
NT = (((1,), (1,)), ((), ()))


def lanes_of(shape):
    return lax.broadcasted_iota(jnp.int32, shape, 1)


def far_is_plus(axis):
    return lax.axis_index(axis) % 2 == 1


def pack_kernel(
    flux, index, count, coupling, state, start, weight, velocity, diffusivity, wet,
    send1, send2, own, index_kept, count_kept, state_kept, start_kept, weight_kept, velocity_kept,
    diffusivity_kept, wet_kept,
    flux_in, coupling_in, index_scr, flux_scr, sems,
):
    pairs = [
        (flux, flux_in), (coupling, coupling_in), (index, index_kept), (count, count_kept), (state, state_kept),
        (start, start_kept), (weight, weight_kept), (velocity, velocity_kept),
        (diffusivity, diffusivity_kept), (wet, wet_kept),
    ]
    copies = [pltpu.make_async_copy(source, target, sems.at[i]) for i, (source, target) in enumerate(pairs)]
    for copy in copies:
        copy.start()
    slots = index.shape[2]
    plus = far_is_plus("row")
    index_scr[...] = jnp.zeros_like(index_scr)
    flux_scr[...] = jnp.zeros_like(flux_scr)
    for copy in copies[:5]:
        copy.wait()
    for i in range(9):
        index_scr[i : i + 1, 0:slots] = index_kept[i]
    size = (8, flux.shape[1])
    terms = [
        jnp.broadcast_to(coupling_in[:, f : f + 1], size) * jnp.broadcast_to(flux_in[f : f + 1, :], size)
        for f in range(flux.shape[0])
    ]
    while len(terms) > 1:
        terms = [sum(terms[i : i + 2]) for i in range(0, len(terms), 2)]
    flux_scr[:, 0 : flux.shape[1]] = terms[0]
    rows = state.shape[0] // 8
    mapped = flux_scr[...]
    lane = lanes_of(mapped.shape)
    west = jnp.zeros_like(mapped)
    east = jnp.zeros_like(mapped)
    width = state.shape[1]
    for y in range(rows):
        line = state_kept[pl.ds(y, 8, stride=rows), :]
        west = jnp.where(lane == y, jnp.broadcast_to(line[:, 0:1], mapped.shape), west)
        east = jnp.where(lane == y, jnp.broadcast_to(line[:, width - 1 : width], mapped.shape), east)
    own[3] = west
    own[4] = east
    groups = []
    for a in range(3):
        for b in range(3):
            used = jnp.broadcast_to(count_kept[a][:, b : b + 1], mapped.shape)
            places = jnp.broadcast_to(index_scr[3 * a + b : 3 * a + b + 1, :], mapped.shape)
            picked = pick(mapped, places)
            flag = ((lane >= OFF) & (lane < OFF + used)).astype(F32)
            groups.append(jnp.where(lane < used, picked, flag))
    for b in range(3):
        up, down = groups[6 + b], groups[b]
        send1[b] = jnp.where(plus, up, down)
        send2[b] = jnp.where(plus, down, up)
        own[b] = groups[3 + b]
    first = state_kept[pl.ds(0, 8, stride=rows), :]
    last = state_kept[pl.ds(rows - 1, 8, stride=rows), :]
    send1[3] = jnp.where(plus, last, first)
    send2[3] = jnp.where(plus, first, last)
    for copy in copies[5:]:
        copy.wait()


def pick(table, lanes):
    return jnp.take_along_axis(table, lanes, axis=1, mode="promise_in_bounds", wrap_negative_indices=False)


def spread_kernel(start, weight, after, matrix, late, start_scr):
    slots, width = weight.shape[3], weight.shape[4]
    start_scr[...] = jnp.zeros_like(start_scr)
    for i in range(9):
        start_scr[i : i + 1, 0:slots] = start[i].astype(F32)
    turned = start_scr[...].T
    lane = lanes_of((slots, width))
    source = lax.broadcasted_iota(jnp.int32, (width, WIN_R * width), 0)
    target = lax.broadcasted_iota(jnp.int32, (width, WIN_R * width), 1)
    wanted = (target // width) * WIN_C + (target & (WIN_C - 1))
    copies = (source == wanted).astype(F32).astype(BF16)
    tops = jnp.concatenate([start[i] // width for i in range(9)], axis=1)
    tops = jnp.broadcast_to(tops, late.shape)
    late[...] = (tops > lax.broadcasted_iota(jnp.int32, late.shape, 0)).astype(F32)
    for i in range(9):
        first = turned[0:slots, i : i + 1].astype(jnp.int32)
        top = first // width
        left = jnp.broadcast_to(first - top * width, (slots, width))
        above = jnp.broadcast_to(top * WIN_C, (slots, width))
        across = lane - left
        inside = (across >= 0) & (across < WIN_C)
        turn = across & (WIN_C - 1)
        group = (lane - above) & (WIN_R * WIN_C - WIN_C)
        block = pick(weight[0, i // 3, i % 3], group + turn)
        part = block.astype(BF16).astype(F32)
        both = jnp.concatenate([part, block - part], axis=0).astype(BF16)
        both = jnp.dot(both, copies, preferred_element_type=F32)
        at_rows = slice(i * slots, (i + 1) * slots)
        for y in range(WIN_R):
            columns = slice(y * width, (y + 1) * width)
            part = jnp.where(inside, both[:slots, columns], 0.0)
            rest = jnp.where(inside, both[slots:, columns], 0.0)
            pair = jnp.concatenate([part, rest], axis=1).astype(BF16)
            matrix[at_rows, 2 * y * width : 2 * (y + 1) * width] = pair


def hot_kernel(index, count, fresh, after, hot, new_state, index_scr, sem):
    store = pltpu.make_async_copy(fresh, new_state, sem)
    store.start()
    slots = index.shape[2]
    cells, width = hot.shape[1], index_scr.shape[1]
    index_scr[...] = jnp.zeros_like(index_scr)
    for i in range(9):
        index_scr[i : i + 1, 0:slots] = index[i]
    lane = lanes_of((1, width))
    used = [lane < jnp.broadcast_to(count[i // 3][:, i % 3 : i % 3 + 1], (1, width)) for i in range(9)]
    places = [jnp.where(used[i], index_scr[i : i + 1, :], -1) for i in range(9)]
    turned = jnp.concatenate(places + [places[0]] * 7, axis=0).astype(F32).T.astype(jnp.int32)
    cell = lanes_of((width, cells))
    for i in range(9):
        here = jnp.broadcast_to(turned[:, i : i + 1], (width, cells)) == cell
        hot[i * width : (i + 1) * width, :] = here.astype(F32).astype(BF16)
    store.wait()


def ocean_kernel(
    row1, row2, col1, col2, own, matrix, late, state, velocity, diffusivity, wet,
    new_state, send1, send2, back_own,
):
    slots = matrix.shape[0] // 9
    width = state.shape[1]
    rows = state.shape[0] // 8
    plus_r = far_is_plus("row")
    plus_c = far_is_plus("col")

    def from_plus(one, two, plus, i):
        return jnp.where(plus, one[i], two[i])

    def from_minus(one, two, plus, i):
        return jnp.where(plus, two[i], one[i])

    middle = [from_minus(row1, row2, plus_r, 1), own[1], from_plus(row1, row2, plus_r, 1)]
    blocks = []
    for p in range(3):
        blocks += [from_minus(col1, col2, plus_c, p), middle[p], from_plus(col1, col2, plus_c, p)]
    south_edge = from_minus(row1, row2, plus_r, 3)
    north_edge = from_plus(row1, row2, plus_r, 3)
    west_edge = from_minus(col1, col2, plus_c, 3)
    east_edge = from_plus(col1, col2, plus_c, 3)

    fields = jnp.concatenate([block[:, 0:slots] for block in blocks], axis=1)
    flags = jnp.concatenate([block[:, OFF : OFF + slots] for block in blocks], axis=1)
    first_row = lax.broadcasted_iota(jnp.int32, flags.shape, 0) == 0
    flags = jnp.where(first_row, flags, 0.0)
    field_high = fields.astype(BF16).astype(F32)
    left = jnp.concatenate([field_high, flags, fields - field_high, jnp.zeros_like(flags)], axis=0)

    lane = lanes_of((8, width))
    row_of = lax.broadcasted_iota(jnp.int32, (8, width), 0)
    one_row = jnp.where(row_of == 0, 1.0, 0.0)
    none = jnp.zeros((8, width), F32)
    spread = none
    for k in range(8):
        spread = jnp.where(row_of == k, jnp.broadcast_to(diffusivity[:, k : k + 1], (8, width)), spread)
    lines = [state[pl.ds(y, 8, stride=rows), :] for y in range(rows)]

    def advance(y, sums):
        forcing = sums[0:8] / jnp.maximum(jnp.broadcast_to(sums[8:9], (8, width)), 1.0)
        here = lines[y]
        north = lines[y + 1] if y + 1 < rows else north_edge
        south = lines[y - 1] if y > 0 else south_edge
        east = pltpu.roll(here, width - 1, 1)
        east = jnp.where(lane == width - 1, jnp.broadcast_to(east_edge[:, y : y + 1], (8, width)), east)
        west = pltpu.roll(here, 1, 1)
        west = jnp.where(lane == 0, jnp.broadcast_to(west_edge[:, y : y + 1], (8, width)), west)
        laplace = east + west + north + south - 4.0 * here
        along = jnp.broadcast_to(velocity[0, y : y + 1, :], (8, width))
        across = jnp.broadcast_to(velocity[1, y : y + 1, :], (8, width))
        advect = 0.5 * (along * (east - west) + across * (north - south))
        mask = jnp.broadcast_to(wet[y : y + 1, :], (8, width)).astype(F32)
        fresh = here + mask * (spread * laplace - advect + forcing)
        new_state[pl.ds(y, 8, stride=rows), :] = fresh
        seen = fresh * mask
        seen_high = seen.astype(BF16).astype(F32)
        return [seen_high, one_row, seen - seen_high, none]

    seen = []
    for y in range(WIN_R):
        moved = jnp.broadcast_to(late[y : y + 1, :], left.shape) > 0
        both = jnp.concatenate([jnp.where(moved, 0.0, left), jnp.where(moved, left, 0.0)], axis=0)
        sums = jnp.dot(
            both.astype(BF16), matrix[:, 2 * y * width : 2 * (y + 1) * width], preferred_element_type=F32
        )
        sums = sums[:, 0:width] + sums[:, width:]
        lines_seen = advance(y, sums[0:16] + sums[16:32])
        lines_seen += advance(y + WIN_R, sums[32:48] + sums[48:64])
        seen.append(jnp.concatenate(lines_seen, axis=0).astype(BF16))
    back = jnp.zeros((16, matrix.shape[0]), F32)
    for y in range(WIN_R):
        moved = jnp.broadcast_to(late[y : y + 1, :], back.shape) > 0
        part = lax.dot_general(
            jnp.concatenate([seen[y], seen[y]], axis=1), matrix[:, 2 * y * width : 2 * (y + 1) * width],
            NT, preferred_element_type=F32,
        )
        back = back + jnp.where(moved, part[32:48] + part[48:64], part[0:16] + part[16:32])
    pad = jnp.zeros((8, OFF - slots), F32)
    out = []
    for i in range(9):
        at = slice(i * slots, (i + 1) * slots)
        out.append(jnp.concatenate([back[0:8, at], pad, back[8:16, at], pad], axis=1))
    for q in range(3):
        up, down = out[6 + q], out[q]
        send1[q] = jnp.where(plus_r, up, down)
        send2[q] = jnp.where(plus_r, down, up)
        back_own[q] = out[3 + q]


def surface_kernel(row1, row2, col1, col2, own, hot, result):
    cells = result.shape[1]
    plus_r = far_is_plus("row")
    plus_c = far_is_plus("col")
    middle = [
        jnp.where(plus_r, row2[1], row1[1]),
        own[1],
        jnp.where(plus_r, row1[1], row2[1]),
    ]
    blocks = []
    for a in range(3):
        blocks += [
            jnp.where(plus_c, col2[a], col1[a]),
            middle[a],
            jnp.where(plus_c, col1[a], col2[a]),
        ]
    values = jnp.concatenate(blocks, axis=1)
    weights = jnp.concatenate([pltpu.roll(block, OFF, 1) for block in blocks], axis=1)
    value_high = values.astype(BF16).astype(F32)
    weight_high = weights.astype(BF16).astype(F32)
    left = jnp.concatenate([value_high, weight_high, values - value_high, weights - weight_high], axis=0)
    total = jnp.dot(left.astype(BF16), hot[...], preferred_element_type=F32)
    total = total[0:16] + total[16:32]
    cover = jnp.maximum(jnp.broadcast_to(total[8:9], (8, cells)), 1.0)
    result[...] = total[0:8] / cover


def swaps(count):
    near = [(i, i ^ 1) for i in range(count)]
    far = [(i, i + 1) for i in range(1, count - 1, 2)]
    far = far + [(j, i) for i, j in far]
    return near, far


def exchange(send1, send2, axis):
    near, far = swaps(lax.axis_size(axis))
    one = lax.ppermute(send1, axis, far)
    send2, _ = lax.optimization_barrier((send2, send1))
    two = lax.ppermute(send2, axis, near)
    return one, two


def column_sends(row1, row2, own, extra, plus_r, plus_c):
    minus = jnp.where(plus_r, row2, row1)
    plus = jnp.where(plus_r, row1, row2)
    low = jnp.stack([minus[0], own[0], plus[0]] + [edge for edge in extra[:1]])
    high = jnp.stack([minus[2], own[2], plus[2]] + [edge for edge in extra[1:]])
    return jnp.where(plus_c, high, low), jnp.where(plus_c, low, high)


def in_hbm(array):
    return pltpu.with_memory_space_constraint(array, pltpu.HBM)


def call(kernel, outs, scratch, specs, flops, size, *args, name, out_specs=None):
    return pl.pallas_call(
        kernel,
        out_shape=outs,
        in_specs=specs,
        out_specs=out_specs or [VMEM] * len(outs),
        scratch_shapes=scratch,
        compiler_params=pltpu.CompilerParams(vmem_limit_bytes=24 * 1024 * 1024),
        cost_estimate=pl.CostEstimate(flops=flops, bytes_accessed=size, transcendentals=0),
        name=name,
    )(*args)


def on_device(
    atm_flux,
    send_index,
    send_count,
    block_start,
    remap_weight,
    coupling,
    ocean_state,
    velocity,
    diffusivity,
    wet_mask,
):
    fields, rows, width = ocean_state.shape
    slots = send_index.shape[3]
    cells = rows * width
    atm_cells = atm_flux.shape[1]
    plus_r = far_is_plus("row")
    plus_c = far_is_plus("col")
    state = ocean_state.reshape(fields * rows, width)
    index = send_index.reshape(9, 1, slots)
    count = send_count.reshape(3, 1, 3)
    start = block_start.reshape(9, 1, slots)

    def shape(*dims, dtype=F32):
        return jax.ShapeDtypeStruct(dims, dtype)

    kept = [index, count, state, start, remap_weight, velocity, diffusivity.reshape(1, -1), wet_mask]
    send1, send2, own, index, count, state, start, weight, velocity, diffusivity, wet = call(
        pack_kernel,
        [shape(4, 8, width), shape(4, 8, width), shape(5, 8, width)]
        + [shape(*array.shape, dtype=array.dtype) for array in kept],
        [
            pltpu.VMEM(atm_flux.shape, F32),
            pltpu.VMEM(coupling.shape, F32),
            pltpu.VMEM((16, width), jnp.int32),
            pltpu.VMEM((8, width), F32),
            pltpu.SemaphoreType.DMA((10,)),
        ],
        [HBM] * 10,
        100_000, 1_000_000,
        *(in_hbm(array) for array in (atm_flux, index, count, coupling)),
        *(in_hbm(array) for array in kept[2:]),
        name="pack",
    )

    def spread(after):
        return call(
            spread_kernel,
            [shape(9 * slots, cells, dtype=BF16), shape(WIN_R, 9 * slots)],
            [pltpu.VMEM((16, width), F32)],
            [VMEM, VMEM, VMEM],
            20_000_000, 4_000_000,
            start, weight, after,
            name="spread",
        )

    row1, row2 = exchange(send1, send2, "row")
    send1, send2 = column_sends(row1, row2, own, [own[3], own[4]], plus_r, plus_c)
    col1, col2 = exchange(send1, send2, "col")
    matrix, late = spread(send1)
    fresh, send1, send2, own = call(
        ocean_kernel,
        [shape(fields * rows, width), shape(3, 8, width), shape(3, 8, width), shape(3, 8, width)],
        [],
        [VMEM] * 11,
        100_000_000, 4_000_000,
        row1, row2, col1, col2, own, matrix, late, state, velocity, diffusivity, wet,
        name="ocean",
    )
    row1, row2 = exchange(send1, send2, "row")
    send1, send2 = column_sends(row1, row2, own, [], plus_r, plus_c)
    col1, col2 = exchange(send1, send2, "col")
    hot, new_state = call(
        hot_kernel,
        [shape(9 * width, atm_cells, dtype=BF16), shape(fields * rows, width)],
        [pltpu.VMEM((16, width), jnp.int32), pltpu.SemaphoreType.DMA],
        [VMEM] * 4,
        1_000_000, 200_000,
        index, count, fresh, send1,
        out_specs=[VMEM, HBM],
        name="hot",
    )
    (result,) = call(
        surface_kernel,
        [shape(fields, atm_cells)],
        [],
        [VMEM] * 6,
        1_000_000, 200_000,
        row1, row2, col1, col2, own, hot,
        name="surface",
    )
    return new_state.reshape(ocean_state.shape), result


def solution(mesh):
    return jax.shard_map(
        on_device,
        mesh=mesh,
        in_specs=(
            P(None, ("row", "col")),
            P(("row", "col"), None, None, None),
            P(("row", "col"), None, None),
            P(("row", "col"), None, None, None),
            P(("row", "col"), None, None, None, None),
            P(),
            P(None, "row", "col"),
            P(None, "row", "col"),
            P(),
            P("row", "col"),
        ),
        out_specs=(P(None, "row", "col"), P(None, ("row", "col"))),
        check_vma=False,
    )
```

```python
import jax
import jax.numpy as jnp
from jax import lax
from jax.experimental import pallas as pl
from jax.experimental.pallas import tpu as pltpu
from jax.sharding import PartitionSpec as P

WIN_R = 8
WIN_C = 16
OFF = 64
VMEM = pl.BlockSpec(memory_space=pltpu.VMEM)
HBM = pl.BlockSpec(memory_space=pltpu.HBM)
F32 = jnp.float32
BF16 = jnp.bfloat16
NT = (((1,), (1,)), ((), ()))


def lanes_of(shape):
    return lax.broadcasted_iota(jnp.int32, shape, 1)


def far_is_plus(axis):
    return lax.axis_index(axis) % 2 == 1


def pack_kernel(
    flux, index, count, coupling, state, start, weight, velocity, diffusivity, wet,
    send1, send2, own, index_kept, count_kept, state_kept, start_kept, weight_kept, velocity_kept,
    diffusivity_kept, wet_kept,
    flux_in, coupling_in, index_scr, flux_scr, sems,
):
    pairs = [
        (flux, flux_in), (coupling, coupling_in), (index, index_kept), (count, count_kept), (state, state_kept),
        (start, start_kept), (weight, weight_kept), (velocity, velocity_kept),
        (diffusivity, diffusivity_kept), (wet, wet_kept),
    ]
    copies = [pltpu.make_async_copy(source, target, sems.at[i]) for i, (source, target) in enumerate(pairs)]
    for copy in copies:
        copy.start()
    slots = index.shape[2]
    plus = far_is_plus("row")
    index_scr[...] = jnp.zeros_like(index_scr)
    flux_scr[...] = jnp.zeros_like(flux_scr)
    for copy in copies[:5]:
        copy.wait()
    for i in range(9):
        index_scr[i : i + 1, 0:slots] = index_kept[i]
    size = (8, flux.shape[1])
    terms = [
        jnp.broadcast_to(coupling_in[:, f : f + 1], size) * jnp.broadcast_to(flux_in[f : f + 1, :], size)
        for f in range(flux.shape[0])
    ]
    while len(terms) > 1:
        terms = [sum(terms[i : i + 2]) for i in range(0, len(terms), 2)]
    flux_scr[:, 0 : flux.shape[1]] = terms[0]
    rows = state.shape[0] // 8
    mapped = flux_scr[...]
    lane = lanes_of(mapped.shape)
    west = jnp.zeros_like(mapped)
    east = jnp.zeros_like(mapped)
    width = state.shape[1]
    for y in range(rows):
        line = state_kept[pl.ds(y, 8, stride=rows), :]
        west = jnp.where(lane == y, jnp.broadcast_to(line[:, 0:1], mapped.shape), west)
        east = jnp.where(lane == y, jnp.broadcast_to(line[:, width - 1 : width], mapped.shape), east)
    own[3] = west
    own[4] = east
    groups = []
    for a in range(3):
        for b in range(3):
            used = jnp.broadcast_to(count_kept[a][:, b : b + 1], mapped.shape)
            places = jnp.broadcast_to(index_scr[3 * a + b : 3 * a + b + 1, :], mapped.shape)
            picked = pick(mapped, places)
            flag = ((lane >= OFF) & (lane < OFF + used)).astype(F32)
            groups.append(jnp.where(lane < used, picked, flag))
    for b in range(3):
        up, down = groups[6 + b], groups[b]
        send1[b] = jnp.where(plus, up, down)
        send2[b] = jnp.where(plus, down, up)
        own[b] = groups[3 + b]
    first = state_kept[pl.ds(0, 8, stride=rows), :]
    last = state_kept[pl.ds(rows - 1, 8, stride=rows), :]
    send1[3] = jnp.where(plus, last, first)
    send2[3] = jnp.where(plus, first, last)
    for copy in copies[5:]:
        copy.wait()


def pick(table, lanes):
    return jnp.take_along_axis(table, lanes, axis=1, mode="promise_in_bounds", wrap_negative_indices=False)


def spread_kernel(start, weight, after, matrix, late, start_scr):
    slots, width = weight.shape[3], weight.shape[4]
    start_scr[...] = jnp.zeros_like(start_scr)
    for i in range(9):
        start_scr[i : i + 1, 0:slots] = start[i].astype(F32)
    turned = start_scr[...].T
    lane = lanes_of((slots, width))
    source = lax.broadcasted_iota(jnp.int32, (width, WIN_R * width), 0)
    target = lax.broadcasted_iota(jnp.int32, (width, WIN_R * width), 1)
    wanted = (target // width) * WIN_C + (target & (WIN_C - 1))
    copies = (source == wanted).astype(F32).astype(BF16)
    tops = jnp.concatenate([start[i] // width for i in range(9)], axis=1)
    tops = jnp.broadcast_to(tops, late.shape)
    late[...] = (tops > lax.broadcasted_iota(jnp.int32, late.shape, 0)).astype(F32)
    for i in range(9):
        first = turned[0:slots, i : i + 1].astype(jnp.int32)
        top = first // width
        left = jnp.broadcast_to(first - top * width, (slots, width))
        above = jnp.broadcast_to(top * WIN_C, (slots, width))
        across = lane - left
        inside = (across >= 0) & (across < WIN_C)
        turn = across & (WIN_C - 1)
        group = (lane - above) & (WIN_R * WIN_C - WIN_C)
        block = pick(weight[0, i // 3, i % 3], group + turn)
        part = block.astype(BF16).astype(F32)
        both = jnp.concatenate([part, block - part], axis=0).astype(BF16)
        both = jnp.dot(both, copies, preferred_element_type=F32)
        at_rows = slice(i * slots, (i + 1) * slots)
        for y in range(WIN_R):
            columns = slice(y * width, (y + 1) * width)
            part = jnp.where(inside, both[:slots, columns], 0.0)
            rest = jnp.where(inside, both[slots:, columns], 0.0)
            pair = jnp.concatenate([part, rest], axis=1).astype(BF16)
            matrix[at_rows, 2 * y * width : 2 * (y + 1) * width] = pair


def hot_kernel(index, count, fresh, hot, new_state, index_scr, sem):
    store = pltpu.make_async_copy(fresh, new_state, sem)
    store.start()
    slots = index.shape[2]
    wide, width = hot.shape[1], index_scr.shape[1]
    index_scr[...] = jnp.full_like(index_scr, -1)
    lane = lanes_of((1, slots))
    for i in range(9):
        used = lane < jnp.broadcast_to(count[i // 3][:, i % 3 : i % 3 + 1], (1, slots))
        index_scr[i : i + 1, 0:slots] = jnp.where(used, index[i], -1)
        index_scr[i : i + 1, OFF : OFF + slots] = jnp.where(used, index[i] + wide // 2, -1)
    turned = index_scr[...].astype(F32).T.astype(jnp.int32)
    cell = lanes_of((width, wide))
    for i in range(9):
        here = jnp.broadcast_to(turned[:, i : i + 1], (width, wide)) == cell
        hot[i * width : (i + 1) * width, :] = here.astype(F32).astype(BF16)
    store.wait()


def ocean_kernel(
    row1, row2, col1, col2, own, matrix, late, state, velocity, diffusivity, wet,
    new_state, send1, send2, back_own,
):
    slots = matrix.shape[0] // 9
    width = state.shape[1]
    rows = state.shape[0] // 8
    plus_r = far_is_plus("row")
    plus_c = far_is_plus("col")

    def from_plus(one, two, plus, i):
        return jnp.where(plus, one[i], two[i])

    def from_minus(one, two, plus, i):
        return jnp.where(plus, two[i], one[i])

    middle = [from_minus(row1, row2, plus_r, 1), own[1], from_plus(row1, row2, plus_r, 1)]
    blocks = []
    for p in range(3):
        blocks += [from_minus(col1, col2, plus_c, p), middle[p], from_plus(col1, col2, plus_c, p)]
    south_edge = from_minus(row1, row2, plus_r, 3)
    north_edge = from_plus(row1, row2, plus_r, 3)
    west_edge = from_minus(col1, col2, plus_c, 3)
    east_edge = from_plus(col1, col2, plus_c, 3)

    fields = jnp.concatenate([block[:, 0:slots] for block in blocks], axis=1)
    flags = jnp.concatenate([block[:, OFF : OFF + slots] for block in blocks], axis=1)
    first_row = lax.broadcasted_iota(jnp.int32, flags.shape, 0) == 0
    flags = jnp.where(first_row, flags, 0.0)
    field_high = fields.astype(BF16).astype(F32)
    left = jnp.concatenate([field_high, flags, fields - field_high, jnp.zeros_like(flags)], axis=0)

    lane = lanes_of((8, width))
    row_of = lax.broadcasted_iota(jnp.int32, (8, width), 0)
    one_row = jnp.where(row_of == 0, 1.0, 0.0)
    none = jnp.zeros((8, width), F32)
    spread = none
    for k in range(8):
        spread = jnp.where(row_of == k, jnp.broadcast_to(diffusivity[:, k : k + 1], (8, width)), spread)
    lines = [state[pl.ds(y, 8, stride=rows), :] for y in range(rows)]

    def advance(y, sums):
        forcing = sums[0:8] / jnp.maximum(jnp.broadcast_to(sums[8:9], (8, width)), 1.0)
        here = lines[y]
        north = lines[y + 1] if y + 1 < rows else north_edge
        south = lines[y - 1] if y > 0 else south_edge
        east = pltpu.roll(here, width - 1, 1)
        east = jnp.where(lane == width - 1, jnp.broadcast_to(east_edge[:, y : y + 1], (8, width)), east)
        west = pltpu.roll(here, 1, 1)
        west = jnp.where(lane == 0, jnp.broadcast_to(west_edge[:, y : y + 1], (8, width)), west)
        laplace = east + west + north + south - 4.0 * here
        along = jnp.broadcast_to(velocity[0, y : y + 1, :], (8, width))
        across = jnp.broadcast_to(velocity[1, y : y + 1, :], (8, width))
        advect = 0.5 * (along * (east - west) + across * (north - south))
        mask = jnp.broadcast_to(wet[y : y + 1, :], (8, width)).astype(F32)
        fresh = here + mask * (spread * laplace - advect + forcing)
        new_state[pl.ds(y, 8, stride=rows), :] = fresh
        seen = fresh * mask
        seen_high = seen.astype(BF16).astype(F32)
        return [seen_high, one_row, seen - seen_high, none]

    seen = []
    for y in range(WIN_R):
        moved = jnp.broadcast_to(late[y : y + 1, :], left.shape) > 0
        both = jnp.concatenate([jnp.where(moved, 0.0, left), jnp.where(moved, left, 0.0)], axis=0)
        sums = jnp.dot(
            both.astype(BF16), matrix[:, 2 * y * width : 2 * (y + 1) * width], preferred_element_type=F32
        )
        sums = sums[:, 0:width] + sums[:, width:]
        lines_seen = advance(y, sums[0:16] + sums[16:32])
        lines_seen += advance(y + WIN_R, sums[32:48] + sums[48:64])
        seen.append(jnp.concatenate(lines_seen, axis=0).astype(BF16))
    back = jnp.zeros((16, matrix.shape[0]), F32)
    for y in range(WIN_R):
        moved = jnp.broadcast_to(late[y : y + 1, :], back.shape) > 0
        part = lax.dot_general(
            jnp.concatenate([seen[y], seen[y]], axis=1), matrix[:, 2 * y * width : 2 * (y + 1) * width],
            NT, preferred_element_type=F32,
        )
        back = back + jnp.where(moved, part[32:48] + part[48:64], part[0:16] + part[16:32])
    pad = jnp.zeros((8, OFF - slots), F32)
    out = []
    for i in range(9):
        at = slice(i * slots, (i + 1) * slots)
        out.append(jnp.concatenate([back[0:8, at], pad, back[8:16, at], pad], axis=1))
    for q in range(3):
        up, down = out[6 + q], out[q]
        send1[q] = jnp.where(plus_r, up, down)
        send2[q] = jnp.where(plus_r, down, up)
        back_own[q] = out[3 + q]


def surface_kernel(row1, row2, col1, col2, own, hot, result):
    cells = result.shape[1]
    plus_r = far_is_plus("row")
    plus_c = far_is_plus("col")
    middle = [
        jnp.where(plus_r, row2[1], row1[1]),
        own[1],
        jnp.where(plus_r, row1[1], row2[1]),
    ]
    blocks = []
    for a in range(3):
        blocks += [
            jnp.where(plus_c, col2[a], col1[a]),
            middle[a],
            jnp.where(plus_c, col1[a], col2[a]),
        ]
    values = jnp.concatenate(blocks, axis=1)
    value_high = values.astype(BF16).astype(F32)
    left = jnp.concatenate([value_high, values - value_high], axis=0).astype(BF16)
    total = jnp.dot(left, hot[...], preferred_element_type=F32)
    total = total[0:8] + total[8:16]
    half = total.shape[1] // 2
    cover = jnp.maximum(jnp.broadcast_to(total[0:1, half : half + cells], (8, cells)), 1.0)
    result[...] = total[:, 0:cells] / cover


def swaps(count):
    near = [(i, i ^ 1) for i in range(count)]
    far = [(i, i + 1) for i in range(1, count - 1, 2)]
    far = far + [(j, i) for i, j in far]
    return near, far


def exchange(send1, send2, axis, far_first=True):
    near, far = swaps(lax.axis_size(axis))
    if far_first:
        send2, _ = lax.optimization_barrier((send2, send1))
    else:
        send1, _ = lax.optimization_barrier((send1, send2))
    one = lax.ppermute(send1, axis, far)
    two = lax.ppermute(send2, axis, near)
    return one, two


def column_sends(row1, row2, own, extra, plus_r, plus_c):
    minus = jnp.where(plus_r, row2, row1)
    plus = jnp.where(plus_r, row1, row2)
    low = jnp.stack([minus[0], own[0], plus[0]] + [edge for edge in extra[:1]])
    high = jnp.stack([minus[2], own[2], plus[2]] + [edge for edge in extra[1:]])
    return jnp.where(plus_c, high, low), jnp.where(plus_c, low, high)


def in_hbm(array):
    return pltpu.with_memory_space_constraint(array, pltpu.HBM)


def call(kernel, outs, scratch, specs, flops, size, *args, name, out_specs=None):
    return pl.pallas_call(
        kernel,
        out_shape=outs,
        in_specs=specs,
        out_specs=out_specs or [VMEM] * len(outs),
        scratch_shapes=scratch,
        compiler_params=pltpu.CompilerParams(vmem_limit_bytes=24 * 1024 * 1024),
        cost_estimate=pl.CostEstimate(flops=flops, bytes_accessed=size, transcendentals=0),
        name=name,
    )(*args)


def on_device(
    atm_flux,
    send_index,
    send_count,
    block_start,
    remap_weight,
    coupling,
    ocean_state,
    velocity,
    diffusivity,
    wet_mask,
):
    fields, rows, width = ocean_state.shape
    slots = send_index.shape[3]
    cells = rows * width
    atm_cells = atm_flux.shape[1]
    plus_r = far_is_plus("row")
    plus_c = far_is_plus("col")
    state = ocean_state.reshape(fields * rows, width)
    index = send_index.reshape(9, 1, slots)
    count = send_count.reshape(3, 1, 3)
    start = block_start.reshape(9, 1, slots)

    def shape(*dims, dtype=F32):
        return jax.ShapeDtypeStruct(dims, dtype)

    kept = [index, count, state, start, remap_weight, velocity, diffusivity.reshape(1, -1), wet_mask]
    send1, send2, own, index, count, state, start, weight, velocity, diffusivity, wet = call(
        pack_kernel,
        [shape(4, 8, width), shape(4, 8, width), shape(5, 8, width)]
        + [shape(*array.shape, dtype=array.dtype) for array in kept],
        [
            pltpu.VMEM(atm_flux.shape, F32),
            pltpu.VMEM(coupling.shape, F32),
            pltpu.VMEM((16, width), jnp.int32),
            pltpu.VMEM((8, width), F32),
            pltpu.SemaphoreType.DMA((10,)),
        ],
        [HBM] * 10,
        100_000, 1_000_000,
        *(in_hbm(array) for array in (atm_flux, index, count, coupling)),
        *(in_hbm(array) for array in kept[2:]),
        name="pack",
    )

    def spread(after):
        return call(
            spread_kernel,
            [shape(9 * slots, cells, dtype=BF16), shape(WIN_R, 9 * slots)],
            [pltpu.VMEM((16, width), F32)],
            [VMEM, VMEM, VMEM],
            20_000_000, 4_000_000,
            start, weight, after,
            name="spread",
        )

    row1, row2 = exchange(send1, send2, "row")
    send1, send2 = column_sends(row1, row2, own, [own[3], own[4]], plus_r, plus_c)
    col1, col2 = exchange(send1, send2, "col")
    matrix, late = spread(send1)
    fresh, send1, send2, own = call(
        ocean_kernel,
        [shape(fields * rows, width), shape(3, 8, width), shape(3, 8, width), shape(3, 8, width)],
        [],
        [VMEM] * 11,
        100_000_000, 4_000_000,
        row1, row2, col1, col2, own, matrix, late, state, velocity, diffusivity, wet,
        name="ocean",
    )
    row1, row2 = exchange(send1, send2, "row", far_first=False)
    hot, new_state = call(
        hot_kernel,
        [shape(9 * width, 2 * width, dtype=BF16), shape(fields * rows, width)],
        [pltpu.VMEM((16, width), jnp.int32), pltpu.SemaphoreType.DMA],
        [VMEM] * 3,
        1_000_000, 200_000,
        index, count, fresh,
        out_specs=[VMEM, HBM],
        name="hot",
    )
    row1, row2, hot = lax.optimization_barrier((row1, row2, hot))
    send1, send2 = column_sends(row1, row2, own, [], plus_r, plus_c)
    col1, col2 = exchange(send1, send2, "col")
    (result,) = call(
        surface_kernel,
        [shape(fields, atm_cells)],
        [],
        [VMEM] * 6,
        1_000_000, 200_000,
        row1, row2, col1, col2, own, hot,
        name="surface",
    )
    return new_state.reshape(ocean_state.shape), result


def solution(mesh):
    return jax.shard_map(
        on_device,
        mesh=mesh,
        in_specs=(
            P(None, ("row", "col")),
            P(("row", "col"), None, None, None),
            P(("row", "col"), None, None),
            P(("row", "col"), None, None, None),
            P(("row", "col"), None, None, None, None),
            P(),
            P(None, "row", "col"),
            P(None, "row", "col"),
            P(),
            P("row", "col"),
        ),
        out_specs=(P(None, "row", "col"), P(None, ("row", "col"))),
        check_vma=False,
    )
```

```python
import jax
import jax.numpy as jnp
from jax import lax
from jax.experimental import pallas as pl
from jax.experimental.pallas import tpu as pltpu
from jax.sharding import PartitionSpec as P

WIN_R = 8
WIN_C = 16
OFF = 64
VMEM = pl.BlockSpec(memory_space=pltpu.VMEM)
HBM = pl.BlockSpec(memory_space=pltpu.HBM)
F32 = jnp.float32
BF16 = jnp.bfloat16
NT = (((1,), (1,)), ((), ()))


def lanes_of(shape):
    return lax.broadcasted_iota(jnp.int32, shape, 1)


def far_is_plus(axis):
    return lax.axis_index(axis) % 2 == 1


def pack_kernel(
    flux, index, count, coupling, state, start, weight, velocity, diffusivity, wet,
    send1, send2, own, index_kept, count_kept, state_kept, start_kept, weight_kept, velocity_kept,
    diffusivity_kept, wet_kept,
    flux_in, coupling_in, index_scr, flux_scr, sems,
):
    pairs = [
        (flux, flux_in), (coupling, coupling_in), (index, index_kept), (count, count_kept), (state, state_kept),
        (start, start_kept), (weight, weight_kept), (velocity, velocity_kept),
        (diffusivity, diffusivity_kept), (wet, wet_kept),
    ]
    copies = [pltpu.make_async_copy(source, target, sems.at[i]) for i, (source, target) in enumerate(pairs)]
    for copy in copies:
        copy.start()
    slots = index.shape[2]
    plus = far_is_plus("col")
    index_scr[...] = jnp.zeros_like(index_scr)
    flux_scr[...] = jnp.zeros_like(flux_scr)
    for copy in copies[:5]:
        copy.wait()
    for i in range(9):
        index_scr[i : i + 1, 0:slots] = index_kept[i]
    size = (8, flux.shape[1])
    terms = [
        jnp.broadcast_to(coupling_in[:, f : f + 1], size) * jnp.broadcast_to(flux_in[f : f + 1, :], size)
        for f in range(flux.shape[0])
    ]
    while len(terms) > 1:
        terms = [sum(terms[i : i + 2]) for i in range(0, len(terms), 2)]
    flux_scr[:, 0 : flux.shape[1]] = terms[0]
    rows = state.shape[0] // 8
    mapped = flux_scr[...]
    lane = lanes_of(mapped.shape)
    west = jnp.zeros_like(mapped)
    east = jnp.zeros_like(mapped)
    width = state.shape[1]
    for y in range(rows):
        line = state_kept[pl.ds(y, 8, stride=rows), :]
        west = jnp.where(lane == y, jnp.broadcast_to(line[:, 0:1], mapped.shape), west)
        east = jnp.where(lane == y, jnp.broadcast_to(line[:, width - 1 : width], mapped.shape), east)
    groups = []
    for a in range(3):
        for b in range(3):
            used = jnp.broadcast_to(count_kept[a][:, b : b + 1], mapped.shape)
            places = jnp.broadcast_to(index_scr[3 * a + b : 3 * a + b + 1, :], mapped.shape)
            picked = pick(mapped, places)
            flag = ((lane >= OFF) & (lane < OFF + used)).astype(F32)
            groups.append(jnp.where(lane < used, picked, flag))
    for a in range(3):
        up, down = groups[3 * a + 2], groups[3 * a]
        send1[a] = jnp.where(plus, up, down)
        send2[a] = jnp.where(plus, down, up)
        own[a] = groups[3 * a + 1]
    send1[3] = jnp.where(plus, east, west)
    send2[3] = jnp.where(plus, west, east)
    own[3] = state_kept[pl.ds(0, 8, stride=rows), :]
    own[4] = state_kept[pl.ds(rows - 1, 8, stride=rows), :]
    for copy in copies[5:]:
        copy.wait()


def pick(table, lanes):
    return jnp.take_along_axis(table, lanes, axis=1, mode="promise_in_bounds", wrap_negative_indices=False)


def spread_kernel(start, weight, after, matrix, late, start_scr):
    slots, width = weight.shape[3], weight.shape[4]
    start_scr[...] = jnp.zeros_like(start_scr)
    for i in range(9):
        start_scr[i : i + 1, 0:slots] = start[i].astype(F32)
    turned = start_scr[...].T
    lane = lanes_of((slots, width))
    source = lax.broadcasted_iota(jnp.int32, (width, WIN_R * width), 0)
    target = lax.broadcasted_iota(jnp.int32, (width, WIN_R * width), 1)
    wanted = (target // width) * WIN_C + (target & (WIN_C - 1))
    copies = (source == wanted).astype(F32).astype(BF16)
    tops = jnp.concatenate([start[i] // width for i in range(9)], axis=1)
    tops = jnp.broadcast_to(tops, late.shape)
    late[...] = (tops > lax.broadcasted_iota(jnp.int32, late.shape, 0)).astype(F32)
    for i in range(9):
        first = turned[0:slots, i : i + 1].astype(jnp.int32)
        top = first // width
        left = jnp.broadcast_to(first - top * width, (slots, width))
        above = jnp.broadcast_to(top * WIN_C, (slots, width))
        across = lane - left
        inside = (across >= 0) & (across < WIN_C)
        turn = across & (WIN_C - 1)
        group = (lane - above) & (WIN_R * WIN_C - WIN_C)
        block = pick(weight[0, i // 3, i % 3], group + turn)
        part = block.astype(BF16).astype(F32)
        both = jnp.concatenate([part, block - part], axis=0).astype(BF16)
        both = jnp.dot(both, copies, preferred_element_type=F32)
        at_rows = slice(i * slots, (i + 1) * slots)
        for y in range(WIN_R):
            columns = slice(y * width, (y + 1) * width)
            part = jnp.where(inside, both[:slots, columns], 0.0)
            rest = jnp.where(inside, both[slots:, columns], 0.0)
            pair = jnp.concatenate([part, rest], axis=1).astype(BF16)
            matrix[at_rows, 2 * y * width : 2 * (y + 1) * width] = pair


def hot_kernel(index, count, fresh, after, hot, new_state, index_scr, sem):
    store = pltpu.make_async_copy(fresh, new_state, sem)
    store.start()
    slots = index.shape[2]
    cells, width = hot.shape[1], index_scr.shape[1]
    index_scr[...] = jnp.zeros_like(index_scr)
    for i in range(9):
        index_scr[i : i + 1, 0:slots] = index[i]
    lane = lanes_of((1, width))
    used = [lane < jnp.broadcast_to(count[i // 3][:, i % 3 : i % 3 + 1], (1, width)) for i in range(9)]
    places = [jnp.where(used[i], index_scr[i : i + 1, :], -1) for i in range(9)]
    turned = jnp.concatenate(places + [places[0]] * 7, axis=0).astype(F32).T.astype(jnp.int32)
    cell = lanes_of((width, cells))
    for i in range(9):
        here = jnp.broadcast_to(turned[:, i : i + 1], (width, cells)) == cell
        hot[i * width : (i + 1) * width, :] = here.astype(F32).astype(BF16)
    store.wait()


def ocean_kernel(
    row1, row2, col1, col2, own, matrix, late, state, velocity, diffusivity, wet,
    new_state, send1, send2, back_own,
):
    slots = matrix.shape[0] // 9
    width = state.shape[1]
    rows = state.shape[0] // 8
    plus_r = far_is_plus("row")
    plus_c = far_is_plus("col")

    def from_plus(one, two, plus, i):
        return jnp.where(plus, one[i], two[i])

    def from_minus(one, two, plus, i):
        return jnp.where(plus, two[i], one[i])

    middle = [from_minus(col1, col2, plus_c, 1), own[1], from_plus(col1, col2, plus_c, 1)]
    blocks = [from_minus(row1, row2, plus_r, q) for q in range(3)]
    blocks += middle
    blocks += [from_plus(row1, row2, plus_r, q) for q in range(3)]
    south_edge = from_minus(row1, row2, plus_r, 3)
    north_edge = from_plus(row1, row2, plus_r, 3)
    west_edge = from_minus(col1, col2, plus_c, 3)
    east_edge = from_plus(col1, col2, plus_c, 3)

    fields = jnp.concatenate([block[:, 0:slots] for block in blocks], axis=1)
    flags = jnp.concatenate([block[:, OFF : OFF + slots] for block in blocks], axis=1)
    first_row = lax.broadcasted_iota(jnp.int32, flags.shape, 0) == 0
    flags = jnp.where(first_row, flags, 0.0)
    field_high = fields.astype(BF16).astype(F32)
    left = jnp.concatenate([field_high, flags, fields - field_high, jnp.zeros_like(flags)], axis=0)

    lane = lanes_of((8, width))
    row_of = lax.broadcasted_iota(jnp.int32, (8, width), 0)
    one_row = jnp.where(row_of == 0, 1.0, 0.0)
    none = jnp.zeros((8, width), F32)
    spread = none
    for k in range(8):
        spread = jnp.where(row_of == k, jnp.broadcast_to(diffusivity[:, k : k + 1], (8, width)), spread)
    lines = [state[pl.ds(y, 8, stride=rows), :] for y in range(rows)]

    def advance(y, sums):
        forcing = sums[0:8] / jnp.maximum(jnp.broadcast_to(sums[8:9], (8, width)), 1.0)
        here = lines[y]
        north = lines[y + 1] if y + 1 < rows else north_edge
        south = lines[y - 1] if y > 0 else south_edge
        east = pltpu.roll(here, width - 1, 1)
        east = jnp.where(lane == width - 1, jnp.broadcast_to(east_edge[:, y : y + 1], (8, width)), east)
        west = pltpu.roll(here, 1, 1)
        west = jnp.where(lane == 0, jnp.broadcast_to(west_edge[:, y : y + 1], (8, width)), west)
        laplace = east + west + north + south - 4.0 * here
        along = jnp.broadcast_to(velocity[0, y : y + 1, :], (8, width))
        across = jnp.broadcast_to(velocity[1, y : y + 1, :], (8, width))
        advect = 0.5 * (along * (east - west) + across * (north - south))
        mask = jnp.broadcast_to(wet[y : y + 1, :], (8, width)).astype(F32)
        fresh = here + mask * (spread * laplace - advect + forcing)
        new_state[pl.ds(y, 8, stride=rows), :] = fresh
        seen = fresh * mask
        seen_high = seen.astype(BF16).astype(F32)
        return [seen_high, one_row, seen - seen_high, none]

    seen = []
    for y in range(WIN_R):
        moved = jnp.broadcast_to(late[y : y + 1, :], left.shape) > 0
        both = jnp.concatenate([jnp.where(moved, 0.0, left), jnp.where(moved, left, 0.0)], axis=0)
        sums = jnp.dot(
            both.astype(BF16), matrix[:, 2 * y * width : 2 * (y + 1) * width], preferred_element_type=F32
        )
        sums = sums[:, 0:width] + sums[:, width:]
        lines_seen = advance(y, sums[0:16] + sums[16:32])
        lines_seen += advance(y + WIN_R, sums[32:48] + sums[48:64])
        seen.append(jnp.concatenate(lines_seen, axis=0).astype(BF16))
    back = jnp.zeros((16, matrix.shape[0]), F32)
    for y in range(WIN_R):
        moved = jnp.broadcast_to(late[y : y + 1, :], back.shape) > 0
        part = lax.dot_general(
            jnp.concatenate([seen[y], seen[y]], axis=1), matrix[:, 2 * y * width : 2 * (y + 1) * width],
            NT, preferred_element_type=F32,
        )
        back = back + jnp.where(moved, part[32:48] + part[48:64], part[0:16] + part[16:32])
    pad = jnp.zeros((8, OFF - slots), F32)
    out = []
    for i in range(9):
        at = slice(i * slots, (i + 1) * slots)
        out.append(jnp.concatenate([back[0:8, at], pad, back[8:16, at], pad], axis=1))
    for q in range(3):
        up, down = out[6 + q], out[q]
        send1[q] = jnp.where(plus_r, up, down)
        send2[q] = jnp.where(plus_r, down, up)
        back_own[q] = out[3 + q]


def surface_kernel(row1, row2, col1, col2, own, hot, result):
    cells = result.shape[1]
    plus_r = far_is_plus("row")
    plus_c = far_is_plus("col")
    middle = [
        jnp.where(plus_r, row2[1], row1[1]),
        own[1],
        jnp.where(plus_r, row1[1], row2[1]),
    ]
    blocks = []
    for a in range(3):
        blocks += [
            jnp.where(plus_c, col2[a], col1[a]),
            middle[a],
            jnp.where(plus_c, col1[a], col2[a]),
        ]
    values = jnp.concatenate(blocks, axis=1)
    weights = jnp.concatenate([pltpu.roll(block, OFF, 1) for block in blocks], axis=1)
    value_high = values.astype(BF16).astype(F32)
    weight_high = weights.astype(BF16).astype(F32)
    left = jnp.concatenate([value_high, weight_high, values - value_high, weights - weight_high], axis=0)
    total = jnp.dot(left.astype(BF16), hot[...], preferred_element_type=F32)
    total = total[0:16] + total[16:32]
    cover = jnp.maximum(jnp.broadcast_to(total[8:9], (8, cells)), 1.0)
    result[...] = total[0:8] / cover


def swaps(count):
    near = [(i, i ^ 1) for i in range(count)]
    far = [(i, i + 1) for i in range(1, count - 1, 2)]
    far = far + [(j, i) for i, j in far]
    return near, far


def exchange(send1, send2, axis):
    near, far = swaps(lax.axis_size(axis))
    one = lax.ppermute(send1, axis, far)
    send2, _ = lax.optimization_barrier((send2, send1))
    two = lax.ppermute(send2, axis, near)
    return one, two


def forward_sends(one, two, own, extra, plus_before, plus_next):
    minus = jnp.where(plus_before, two, one)
    plus = jnp.where(plus_before, one, two)
    low = jnp.stack([minus[0], own[0], plus[0]] + extra[:1])
    high = jnp.stack([minus[2], own[2], plus[2]] + extra[1:])
    return jnp.where(plus_next, high, low), jnp.where(plus_next, low, high)


def in_hbm(array):
    return pltpu.with_memory_space_constraint(array, pltpu.HBM)


def call(kernel, outs, scratch, specs, flops, size, *args, name, out_specs=None):
    return pl.pallas_call(
        kernel,
        out_shape=outs,
        in_specs=specs,
        out_specs=out_specs or [VMEM] * len(outs),
        scratch_shapes=scratch,
        compiler_params=pltpu.CompilerParams(vmem_limit_bytes=24 * 1024 * 1024),
        cost_estimate=pl.CostEstimate(flops=flops, bytes_accessed=size, transcendentals=0),
        name=name,
    )(*args)


def on_device(
    atm_flux,
    send_index,
    send_count,
    block_start,
    remap_weight,
    coupling,
    ocean_state,
    velocity,
    diffusivity,
    wet_mask,
):
    fields, rows, width = ocean_state.shape
    slots = send_index.shape[3]
    cells = rows * width
    atm_cells = atm_flux.shape[1]
    plus_r = far_is_plus("row")
    plus_c = far_is_plus("col")
    state = ocean_state.reshape(fields * rows, width)
    index = send_index.reshape(9, 1, slots)
    count = send_count.reshape(3, 1, 3)
    start = block_start.reshape(9, 1, slots)

    def shape(*dims, dtype=F32):
        return jax.ShapeDtypeStruct(dims, dtype)

    kept = [index, count, state, start, remap_weight, velocity, diffusivity.reshape(1, -1), wet_mask]
    send1, send2, own, index, count, state, start, weight, velocity, diffusivity, wet = call(
        pack_kernel,
        [shape(4, 8, width), shape(4, 8, width), shape(5, 8, width)]
        + [shape(*array.shape, dtype=array.dtype) for array in kept],
        [
            pltpu.VMEM(atm_flux.shape, F32),
            pltpu.VMEM(coupling.shape, F32),
            pltpu.VMEM((16, width), jnp.int32),
            pltpu.VMEM((8, width), F32),
            pltpu.SemaphoreType.DMA((10,)),
        ],
        [HBM] * 10,
        100_000, 1_000_000,
        *(in_hbm(array) for array in (atm_flux, index, count, coupling)),
        *(in_hbm(array) for array in kept[2:]),
        name="pack",
    )

    def spread(after):
        return call(
            spread_kernel,
            [shape(9 * slots, cells, dtype=BF16), shape(WIN_R, 9 * slots)],
            [pltpu.VMEM((16, width), F32)],
            [VMEM, VMEM, VMEM],
            20_000_000, 4_000_000,
            start, weight, after,
            name="spread",
        )

    col1, col2 = exchange(send1, send2, "col")
    matrix, late = spread(own)
    col1, col2, matrix = lax.optimization_barrier((col1, col2, matrix))
    send1, send2 = forward_sends(col1, col2, own, [own[3], own[4]], plus_c, plus_r)
    row1, row2 = exchange(send1, send2, "row")
    fresh, send1, send2, own = call(
        ocean_kernel,
        [shape(fields * rows, width), shape(3, 8, width), shape(3, 8, width), shape(3, 8, width)],
        [],
        [VMEM] * 11,
        100_000_000, 4_000_000,
        row1, row2, col1, col2, own, matrix, late, state, velocity, diffusivity, wet,
        name="ocean",
    )
    row1, row2 = exchange(send1, send2, "row")
    send1, send2 = forward_sends(row1, row2, own, [], plus_r, plus_c)
    col1, col2 = exchange(send1, send2, "col")
    hot, new_state = call(
        hot_kernel,
        [shape(9 * width, atm_cells, dtype=BF16), shape(fields * rows, width)],
        [pltpu.VMEM((16, width), jnp.int32), pltpu.SemaphoreType.DMA],
        [VMEM] * 4,
        1_000_000, 200_000,
        index, count, fresh, send1,
        out_specs=[VMEM, HBM],
        name="hot",
    )
    (result,) = call(
        surface_kernel,
        [shape(fields, atm_cells)],
        [],
        [VMEM] * 6,
        1_000_000, 200_000,
        row1, row2, col1, col2, own, hot,
        name="surface",
    )
    return new_state.reshape(ocean_state.shape), result


def solution(mesh):
    return jax.shard_map(
        on_device,
        mesh=mesh,
        in_specs=(
            P(None, ("row", "col")),
            P(("row", "col"), None, None, None),
            P(("row", "col"), None, None),
            P(("row", "col"), None, None, None),
            P(("row", "col"), None, None, None, None),
            P(),
            P(None, "row", "col"),
            P(None, "row", "col"),
            P(),
            P("row", "col"),
        ),
        out_specs=(P(None, "row", "col"), P(None, ("row", "col"))),
        check_vma=False,
    )
```

```python
import jax
import jax.numpy as jnp
from jax import lax
from jax.experimental import pallas as pl
from jax.experimental.pallas import tpu as pltpu
from jax.sharding import PartitionSpec as P

WIN_R = 8
WIN_C = 16
OFF = 64
VMEM = pl.BlockSpec(memory_space=pltpu.VMEM)
HBM = pl.BlockSpec(memory_space=pltpu.HBM)
F32 = jnp.float32
BF16 = jnp.bfloat16
NT = (((1,), (1,)), ((), ()))


def lanes_of(shape):
    return lax.broadcasted_iota(jnp.int32, shape, 1)


def far_is_plus(axis):
    return lax.axis_index(axis) % 2 == 1


def pack_kernel(
    flux, index, count, coupling, state, start, weight, velocity, diffusivity, wet,
    send1, send2, own, index_kept, count_kept, state_kept, start_kept, weight_kept, velocity_kept,
    diffusivity_kept, wet_kept,
    flux_in, coupling_in, index_scr, flux_scr, sems,
):
    pairs = [
        (flux, flux_in), (coupling, coupling_in), (index, index_kept), (count, count_kept), (state, state_kept),
        (start, start_kept), (weight, weight_kept), (velocity, velocity_kept),
        (diffusivity, diffusivity_kept), (wet, wet_kept),
    ]
    copies = [pltpu.make_async_copy(source, target, sems.at[i]) for i, (source, target) in enumerate(pairs)]
    for copy in copies:
        copy.start()
    slots = index.shape[2]
    plus = far_is_plus("row")
    index_scr[...] = jnp.zeros_like(index_scr)
    flux_scr[...] = jnp.zeros_like(flux_scr)
    for copy in copies[:5]:
        copy.wait()
    for i in range(9):
        index_scr[i : i + 1, 0:slots] = index_kept[i]
    size = (8, flux.shape[1])
    terms = [
        jnp.broadcast_to(coupling_in[:, f : f + 1], size) * jnp.broadcast_to(flux_in[f : f + 1, :], size)
        for f in range(flux.shape[0])
    ]
    while len(terms) > 1:
        terms = [sum(terms[i : i + 2]) for i in range(0, len(terms), 2)]
    flux_scr[:, 0 : flux.shape[1]] = terms[0]
    rows = state.shape[0] // 8
    mapped = flux_scr[...]
    lane = lanes_of(mapped.shape)
    west = jnp.zeros_like(mapped)
    east = jnp.zeros_like(mapped)
    width = state.shape[1]
    for y in range(rows):
        line = state_kept[pl.ds(y, 8, stride=rows), :]
        west = jnp.where(lane == y, jnp.broadcast_to(line[:, 0:1], mapped.shape), west)
        east = jnp.where(lane == y, jnp.broadcast_to(line[:, width - 1 : width], mapped.shape), east)
    own[3] = west
    own[4] = east
    groups = []
    for a in range(3):
        for b in range(3):
            used = jnp.broadcast_to(count_kept[a][:, b : b + 1], mapped.shape)
            places = jnp.broadcast_to(index_scr[3 * a + b : 3 * a + b + 1, :], mapped.shape)
            picked = pick(mapped, places)
            flag = ((lane >= OFF) & (lane < OFF + used)).astype(F32)
            groups.append(jnp.where(lane < used, picked, flag))
    for b in range(3):
        up, down = groups[6 + b], groups[b]
        send1[b] = jnp.where(plus, up, down)
        send2[b] = jnp.where(plus, down, up)
        own[b] = groups[3 + b]
    first = state_kept[pl.ds(0, 8, stride=rows), :]
    last = state_kept[pl.ds(rows - 1, 8, stride=rows), :]
    send1[3] = jnp.where(plus, last, first)
    send2[3] = jnp.where(plus, first, last)
    for copy in copies[5:]:
        copy.wait()


def pick(table, lanes):
    return jnp.take_along_axis(table, lanes, axis=1, mode="promise_in_bounds", wrap_negative_indices=False)


def spread_kernel(start, weight, after, matrix, late, start_scr):
    slots, width = weight.shape[3], weight.shape[4]
    start_scr[...] = jnp.zeros_like(start_scr)
    for i in range(9):
        start_scr[i : i + 1, 0:slots] = start[i].astype(F32)
    turned = start_scr[...].T
    lane = lanes_of((slots, width))
    source = lax.broadcasted_iota(jnp.int32, (width, WIN_R * width), 0)
    target = lax.broadcasted_iota(jnp.int32, (width, WIN_R * width), 1)
    wanted = (target // width) * WIN_C + (target & (WIN_C - 1))
    copies = (source == wanted).astype(F32).astype(BF16)
    tops = jnp.concatenate([start[i] // width for i in range(9)], axis=1)
    tops = jnp.broadcast_to(tops, late.shape)
    late[...] = (tops > lax.broadcasted_iota(jnp.int32, late.shape, 0)).astype(F32)
    for i in range(9):
        first = turned[0:slots, i : i + 1].astype(jnp.int32)
        top = first // width
        left = jnp.broadcast_to(first - top * width, (slots, width))
        above = jnp.broadcast_to(top * WIN_C, (slots, width))
        across = lane - left
        inside = (across >= 0) & (across < WIN_C)
        turn = across & (WIN_C - 1)
        group = (lane - above) & (WIN_R * WIN_C - WIN_C)
        block = pick(weight[0, i // 3, i % 3], group + turn)
        part = block.astype(BF16).astype(F32)
        both = jnp.concatenate([part, block - part], axis=0).astype(BF16)
        both = jnp.dot(both, copies, preferred_element_type=F32)
        at_rows = slice(i * slots, (i + 1) * slots)
        for y in range(WIN_R):
            columns = slice(y * width, (y + 1) * width)
            part = jnp.where(inside, both[:slots, columns], 0.0)
            rest = jnp.where(inside, both[slots:, columns], 0.0)
            pair = jnp.concatenate([part, rest], axis=1).astype(BF16)
            matrix[at_rows, 2 * y * width : 2 * (y + 1) * width] = pair


def hot_kernel(index, count, fresh, hot, new_state, index_scr, sem):
    store = pltpu.make_async_copy(fresh, new_state, sem)
    store.start()
    slots = index.shape[2]
    wide, width = hot.shape[1], index_scr.shape[1]
    index_scr[...] = jnp.full_like(index_scr, -1)
    lane = lanes_of((1, slots))
    for i in range(9):
        used = lane < jnp.broadcast_to(count[i // 3][:, i % 3 : i % 3 + 1], (1, slots))
        index_scr[i : i + 1, 0:slots] = jnp.where(used, index[i], -1)
        index_scr[i : i + 1, OFF : OFF + slots] = jnp.where(used, index[i] + wide // 2, -1)
    turned = index_scr[...].astype(F32).T.astype(jnp.int32)
    cell = lanes_of((width, wide))
    for i in range(9):
        here = jnp.broadcast_to(turned[:, i : i + 1], (width, wide)) == cell
        hot[i * width : (i + 1) * width, :] = here.astype(F32).astype(BF16)
    store.wait()


def ocean_kernel(
    row1, row2, col1, col2, own, matrix, late, state, velocity, diffusivity, wet,
    new_state, send1, send2, back_own,
):
    slots = matrix.shape[0] // 9
    width = state.shape[1]
    rows = state.shape[0] // 8
    plus_r = far_is_plus("row")
    plus_c = far_is_plus("col")

    def from_plus(one, two, plus, i):
        return jnp.where(plus, one[i], two[i])

    def from_minus(one, two, plus, i):
        return jnp.where(plus, two[i], one[i])

    middle = [from_minus(row1, row2, plus_r, 1), own[1], from_plus(row1, row2, plus_r, 1)]
    blocks = []
    for p in range(3):
        blocks += [from_minus(col1, col2, plus_c, p), middle[p], from_plus(col1, col2, plus_c, p)]
    south_edge = from_minus(row1, row2, plus_r, 3)
    north_edge = from_plus(row1, row2, plus_r, 3)
    west_edge = from_minus(col1, col2, plus_c, 3)
    east_edge = from_plus(col1, col2, plus_c, 3)

    fields = jnp.concatenate([block[:, 0:slots] for block in blocks], axis=1)
    flags = jnp.concatenate([block[:, OFF : OFF + slots] for block in blocks], axis=1)
    first_row = lax.broadcasted_iota(jnp.int32, flags.shape, 0) == 0
    flags = jnp.where(first_row, flags, 0.0)
    field_high = fields.astype(BF16).astype(F32)
    left = jnp.concatenate([field_high, flags, fields - field_high, jnp.zeros_like(flags)], axis=0)

    lane = lanes_of((8, width))
    row_of = lax.broadcasted_iota(jnp.int32, (8, width), 0)
    one_row = jnp.where(row_of == 0, 1.0, 0.0)
    none = jnp.zeros((8, width), F32)
    spread = none
    for k in range(8):
        spread = jnp.where(row_of == k, jnp.broadcast_to(diffusivity[:, k : k + 1], (8, width)), spread)
    lines = [state[pl.ds(y, 8, stride=rows), :] for y in range(rows)]

    def advance(y, sums):
        forcing = sums[0:8] / jnp.maximum(jnp.broadcast_to(sums[8:9], (8, width)), 1.0)
        here = lines[y]
        north = lines[y + 1] if y + 1 < rows else north_edge
        south = lines[y - 1] if y > 0 else south_edge
        east = pltpu.roll(here, width - 1, 1)
        east = jnp.where(lane == width - 1, jnp.broadcast_to(east_edge[:, y : y + 1], (8, width)), east)
        west = pltpu.roll(here, 1, 1)
        west = jnp.where(lane == 0, jnp.broadcast_to(west_edge[:, y : y + 1], (8, width)), west)
        laplace = east + west + north + south - 4.0 * here
        along = jnp.broadcast_to(velocity[0, y : y + 1, :], (8, width))
        across = jnp.broadcast_to(velocity[1, y : y + 1, :], (8, width))
        advect = 0.5 * (along * (east - west) + across * (north - south))
        mask = jnp.broadcast_to(wet[y : y + 1, :], (8, width)).astype(F32)
        fresh = here + mask * (spread * laplace - advect + forcing)
        new_state[pl.ds(y, 8, stride=rows), :] = fresh
        seen = fresh * mask
        seen_high = seen.astype(BF16).astype(F32)
        return [seen_high, one_row, seen - seen_high, none]

    seen = []
    for y in range(WIN_R):
        moved = jnp.broadcast_to(late[y : y + 1, :], left.shape) > 0
        both = jnp.concatenate([jnp.where(moved, 0.0, left), jnp.where(moved, left, 0.0)], axis=0)
        sums = jnp.dot(
            both.astype(BF16), matrix[:, 2 * y * width : 2 * (y + 1) * width], preferred_element_type=F32
        )
        sums = sums[:, 0:width] + sums[:, width:]
        lines_seen = advance(y, sums[0:16] + sums[16:32])
        lines_seen += advance(y + WIN_R, sums[32:48] + sums[48:64])
        seen.append(jnp.concatenate(lines_seen, axis=0).astype(BF16))
    back = jnp.zeros((16, matrix.shape[0]), F32)
    for y in range(WIN_R):
        moved = jnp.broadcast_to(late[y : y + 1, :], back.shape) > 0
        part = lax.dot_general(
            jnp.concatenate([seen[y], seen[y]], axis=1), matrix[:, 2 * y * width : 2 * (y + 1) * width],
            NT, preferred_element_type=F32,
        )
        back = back + jnp.where(moved, part[32:48] + part[48:64], part[0:16] + part[16:32])
    pad = jnp.zeros((8, OFF - slots), F32)
    out = []
    for i in range(9):
        at = slice(i * slots, (i + 1) * slots)
        out.append(jnp.concatenate([back[0:8, at], pad, back[8:16, at], pad], axis=1))
    for q in range(3):
        up, down = out[6 + q], out[q]
        send1[q] = jnp.where(plus_r, up, down)
        send2[q] = jnp.where(plus_r, down, up)
        back_own[q] = out[3 + q]


def surface_kernel(row1, row2, col1, col2, own, hot, result):
    cells = result.shape[1]
    plus_r = far_is_plus("row")
    plus_c = far_is_plus("col")
    middle = [
        jnp.where(plus_r, row2[1], row1[1]),
        own[1],
        jnp.where(plus_r, row1[1], row2[1]),
    ]
    blocks = []
    for a in range(3):
        blocks += [
            jnp.where(plus_c, col2[a], col1[a]),
            middle[a],
            jnp.where(plus_c, col1[a], col2[a]),
        ]
    values = jnp.concatenate(blocks, axis=1)
    value_high = values.astype(BF16).astype(F32)
    left = jnp.concatenate([value_high, values - value_high], axis=0).astype(BF16)
    total = jnp.dot(left, hot[...], preferred_element_type=F32)
    total = total[0:8] + total[8:16]
    half = total.shape[1] // 2
    cover = jnp.maximum(jnp.broadcast_to(total[0:1, half : half + cells], (8, cells)), 1.0)
    result[...] = total[:, 0:cells] / cover


def swaps(count):
    near = [(i, i ^ 1) for i in range(count)]
    far = [(i, i + 1) for i in range(1, count - 1, 2)]
    far = far + [(j, i) for i, j in far]
    return near, far


def exchange(send1, send2, axis):
    near, far = swaps(lax.axis_size(axis))
    one = lax.ppermute(send1, axis, far)
    send2, _ = lax.optimization_barrier((send2, send1))
    two = lax.ppermute(send2, axis, near)
    return one, two


def column_sends(row1, row2, own, extra, plus_r, plus_c):
    minus = jnp.where(plus_r, row2, row1)
    plus = jnp.where(plus_r, row1, row2)
    low = jnp.stack([minus[0], own[0], plus[0]] + [edge for edge in extra[:1]])
    high = jnp.stack([minus[2], own[2], plus[2]] + [edge for edge in extra[1:]])
    return jnp.where(plus_c, high, low), jnp.where(plus_c, low, high)


def in_hbm(array):
    return pltpu.with_memory_space_constraint(array, pltpu.HBM)


def call(kernel, outs, scratch, specs, flops, size, *args, name, out_specs=None):
    return pl.pallas_call(
        kernel,
        out_shape=outs,
        in_specs=specs,
        out_specs=out_specs or [VMEM] * len(outs),
        scratch_shapes=scratch,
        compiler_params=pltpu.CompilerParams(vmem_limit_bytes=24 * 1024 * 1024),
        cost_estimate=pl.CostEstimate(flops=flops, bytes_accessed=size, transcendentals=0),
        name=name,
    )(*args)


def on_device(
    atm_flux,
    send_index,
    send_count,
    block_start,
    remap_weight,
    coupling,
    ocean_state,
    velocity,
    diffusivity,
    wet_mask,
):
    fields, rows, width = ocean_state.shape
    slots = send_index.shape[3]
    cells = rows * width
    atm_cells = atm_flux.shape[1]
    plus_r = far_is_plus("row")
    plus_c = far_is_plus("col")
    state = ocean_state.reshape(fields * rows, width)
    index = send_index.reshape(9, 1, slots)
    count = send_count.reshape(3, 1, 3)
    start = block_start.reshape(9, 1, slots)

    def shape(*dims, dtype=F32):
        return jax.ShapeDtypeStruct(dims, dtype)

    kept = [index, count, state, start, remap_weight, velocity, diffusivity.reshape(1, -1), wet_mask]
    send1, send2, own, index, count, state, start, weight, velocity, diffusivity, wet = call(
        pack_kernel,
        [shape(4, 8, width), shape(4, 8, width), shape(5, 8, width)]
        + [shape(*array.shape, dtype=array.dtype) for array in kept],
        [
            pltpu.VMEM(atm_flux.shape, F32),
            pltpu.VMEM(coupling.shape, F32),
            pltpu.VMEM((16, width), jnp.int32),
            pltpu.VMEM((8, width), F32),
            pltpu.SemaphoreType.DMA((10,)),
        ],
        [HBM] * 10,
        100_000, 1_000_000,
        *(in_hbm(array) for array in (atm_flux, index, count, coupling)),
        *(in_hbm(array) for array in kept[2:]),
        name="pack",
    )

    def spread(after):
        return call(
            spread_kernel,
            [shape(9 * slots, cells, dtype=BF16), shape(WIN_R, 9 * slots)],
            [pltpu.VMEM((16, width), F32)],
            [VMEM, VMEM, VMEM],
            20_000_000, 4_000_000,
            start, weight, after,
            name="spread",
        )

    row1, row2 = exchange(send1, send2, "row")
    send1, send2 = column_sends(row1, row2, own, [own[3], own[4]], plus_r, plus_c)
    col1, col2 = exchange(send1, send2, "col")
    matrix, late = spread(send1)
    fresh, send1, send2, own = call(
        ocean_kernel,
        [shape(fields * rows, width), shape(3, 8, width), shape(3, 8, width), shape(3, 8, width)],
        [],
        [VMEM] * 11,
        100_000_000, 4_000_000,
        row1, row2, col1, col2, own, matrix, late, state, velocity, diffusivity, wet,
        name="ocean",
    )
    row1, row2 = exchange(send1, send2, "row")
    hot, new_state = call(
        hot_kernel,
        [shape(9 * width, 2 * width, dtype=BF16), shape(fields * rows, width)],
        [pltpu.VMEM((16, width), jnp.int32), pltpu.SemaphoreType.DMA],
        [VMEM] * 3,
        1_000_000, 200_000,
        index, count, fresh,
        out_specs=[VMEM, HBM],
        name="hot",
    )
    row1, row2, hot = lax.optimization_barrier((row1, row2, hot))
    send1, send2 = column_sends(row1, row2, own, [], plus_r, plus_c)
    col1, col2 = exchange(send1, send2, "col")
    (result,) = call(
        surface_kernel,
        [shape(fields, atm_cells)],
        [],
        [VMEM] * 6,
        1_000_000, 200_000,
        row1, row2, col1, col2, own, hot,
        name="surface",
    )
    return new_state.reshape(ocean_state.shape), result


def solution(mesh):
    return jax.shard_map(
        on_device,
        mesh=mesh,
        in_specs=(
            P(None, ("row", "col")),
            P(("row", "col"), None, None, None),
            P(("row", "col"), None, None),
            P(("row", "col"), None, None, None),
            P(("row", "col"), None, None, None, None),
            P(),
            P(None, "row", "col"),
            P(None, "row", "col"),
            P(),
            P("row", "col"),
        ),
        out_specs=(P(None, "row", "col"), P(None, ("row", "col"))),
        check_vma=False,
    )
```

```python
import jax
import jax.numpy as jnp
from jax import lax
from jax.experimental import pallas as pl
from jax.experimental.pallas import tpu as pltpu
from jax.sharding import PartitionSpec as P

WIN_R = 8
WIN_C = 16
OFF = 64
VMEM = pl.BlockSpec(memory_space=pltpu.VMEM)
HBM = pl.BlockSpec(memory_space=pltpu.HBM)
F32 = jnp.float32
BF16 = jnp.bfloat16
NT = (((1,), (1,)), ((), ()))


def lanes_of(shape):
    return lax.broadcasted_iota(jnp.int32, shape, 1)


def far_is_plus(axis):
    return lax.axis_index(axis) % 2 == 1


def pack_kernel(
    flux, index, count, coupling, state, start, weight, velocity, diffusivity, wet,
    send1, send2, own, index_kept, count_kept, state_kept, start_kept, weight_kept, velocity_kept,
    diffusivity_kept, wet_kept,
    flux_in, coupling_in, index_scr, flux_scr, sems,
):
    pairs = [
        (flux, flux_in), (coupling, coupling_in), (index, index_kept), (count, count_kept), (state, state_kept),
        (start, start_kept), (weight, weight_kept), (velocity, velocity_kept),
        (diffusivity, diffusivity_kept), (wet, wet_kept),
    ]
    copies = [pltpu.make_async_copy(source, target, sems.at[i]) for i, (source, target) in enumerate(pairs)]
    for copy in copies:
        copy.start()
    slots = index.shape[2]
    plus = far_is_plus("row")
    index_scr[...] = jnp.zeros_like(index_scr)
    flux_scr[...] = jnp.zeros_like(flux_scr)
    for copy in copies[:5]:
        copy.wait()
    for i in range(9):
        index_scr[i : i + 1, 0:slots] = index_kept[i]
    size = (8, flux.shape[1])
    terms = [
        jnp.broadcast_to(coupling_in[:, f : f + 1], size) * jnp.broadcast_to(flux_in[f : f + 1, :], size)
        for f in range(flux.shape[0])
    ]
    while len(terms) > 1:
        terms = [sum(terms[i : i + 2]) for i in range(0, len(terms), 2)]
    flux_scr[:, 0 : flux.shape[1]] = terms[0]
    rows = state.shape[0] // 8
    mapped = flux_scr[...]
    lane = lanes_of(mapped.shape)
    west = jnp.zeros_like(mapped)
    east = jnp.zeros_like(mapped)
    width = state.shape[1]
    for y in range(rows):
        line = state_kept[pl.ds(y, 8, stride=rows), :]
        west = jnp.where(lane == y, jnp.broadcast_to(line[:, 0:1], mapped.shape), west)
        east = jnp.where(lane == y, jnp.broadcast_to(line[:, width - 1 : width], mapped.shape), east)
    own[3] = west
    own[4] = east
    groups = []
    for a in range(3):
        for b in range(3):
            used = jnp.broadcast_to(count_kept[a][:, b : b + 1], mapped.shape)
            places = jnp.broadcast_to(index_scr[3 * a + b : 3 * a + b + 1, :], mapped.shape)
            picked = pick(mapped, places)
            flag = ((lane >= OFF) & (lane < OFF + used)).astype(F32)
            groups.append(jnp.where(lane < used, picked, flag))
    for b in range(3):
        up, down = groups[6 + b], groups[b]
        send1[b] = jnp.where(plus, up, down)
        send2[b] = jnp.where(plus, down, up)
        own[b] = groups[3 + b]
    first = state_kept[pl.ds(0, 8, stride=rows), :]
    last = state_kept[pl.ds(rows - 1, 8, stride=rows), :]
    send1[3] = jnp.where(plus, last, first)
    send2[3] = jnp.where(plus, first, last)
    for copy in copies[5:]:
        copy.wait()


def pick(table, lanes):
    return jnp.take_along_axis(table, lanes, axis=1, mode="promise_in_bounds", wrap_negative_indices=False)


def spread_kernel(start, weight, after, matrix, late, start_scr):
    slots, width = weight.shape[3], weight.shape[4]
    start_scr[...] = jnp.zeros_like(start_scr)
    for i in range(9):
        start_scr[i : i + 1, 0:slots] = start[i].astype(F32)
    turned = start_scr[...].T
    lane = lanes_of((slots, width))
    source = lax.broadcasted_iota(jnp.int32, (width, WIN_R * width), 0)
    target = lax.broadcasted_iota(jnp.int32, (width, WIN_R * width), 1)
    wanted = (target // width) * WIN_C + (target & (WIN_C - 1))
    copies = (source == wanted).astype(F32).astype(BF16)
    tops = jnp.concatenate([start[i] // width for i in range(9)], axis=1)
    tops = jnp.broadcast_to(tops, late.shape)
    late[...] = (tops > lax.broadcasted_iota(jnp.int32, late.shape, 0)).astype(F32)
    for i in range(9):
        first = turned[0:slots, i : i + 1].astype(jnp.int32)
        top = first // width
        left = jnp.broadcast_to(first - top * width, (slots, width))
        above = jnp.broadcast_to(top * WIN_C, (slots, width))
        across = lane - left
        inside = (across >= 0) & (across < WIN_C)
        turn = across & (WIN_C - 1)
        group = (lane - above) & (WIN_R * WIN_C - WIN_C)
        block = pick(weight[0, i // 3, i % 3], group + turn)
        part = block.astype(BF16).astype(F32)
        both = jnp.concatenate([part, block - part], axis=0).astype(BF16)
        both = jnp.dot(both, copies, preferred_element_type=F32)
        at_rows = slice(i * slots, (i + 1) * slots)
        for y in range(WIN_R):
            columns = slice(y * width, (y + 1) * width)
            part = jnp.where(inside, both[:slots, columns], 0.0)
            rest = jnp.where(inside, both[slots:, columns], 0.0)
            pair = jnp.concatenate([part, rest], axis=1).astype(BF16)
            matrix[at_rows, 2 * y * width : 2 * (y + 1) * width] = pair


def hot_kernel(index, count, fresh, after, hot, new_state, index_scr, sem):
    store = pltpu.make_async_copy(fresh, new_state, sem)
    store.start()
    slots = index.shape[2]
    wide, width = hot.shape[1], index_scr.shape[1]
    index_scr[...] = jnp.full_like(index_scr, -1)
    lane = lanes_of((1, slots))
    for i in range(9):
        used = lane < jnp.broadcast_to(count[i // 3][:, i % 3 : i % 3 + 1], (1, slots))
        index_scr[i : i + 1, 0:slots] = jnp.where(used, index[i], -1)
        index_scr[i : i + 1, OFF : OFF + slots] = jnp.where(used, index[i] + wide // 2, -1)
    turned = index_scr[...].astype(F32).T.astype(jnp.int32)
    cell = lanes_of((width, wide))
    for i in range(9):
        here = jnp.broadcast_to(turned[:, i : i + 1], (width, wide)) == cell
        hot[i * width : (i + 1) * width, :] = here.astype(F32).astype(BF16)
    store.wait()


def ocean_kernel(
    row1, row2, col1, col2, own, matrix, late, state, velocity, diffusivity, wet,
    new_state, send1, send2, back_own,
):
    slots = matrix.shape[0] // 9
    width = state.shape[1]
    rows = state.shape[0] // 8
    plus_r = far_is_plus("row")
    plus_c = far_is_plus("col")

    def from_plus(one, two, plus, i):
        return jnp.where(plus, one[i], two[i])

    def from_minus(one, two, plus, i):
        return jnp.where(plus, two[i], one[i])

    middle = [from_minus(row1, row2, plus_r, 1), own[1], from_plus(row1, row2, plus_r, 1)]
    blocks = []
    for p in range(3):
        blocks += [from_minus(col1, col2, plus_c, p), middle[p], from_plus(col1, col2, plus_c, p)]
    south_edge = from_minus(row1, row2, plus_r, 3)
    north_edge = from_plus(row1, row2, plus_r, 3)
    west_edge = from_minus(col1, col2, plus_c, 3)
    east_edge = from_plus(col1, col2, plus_c, 3)

    fields = jnp.concatenate([block[:, 0:slots] for block in blocks], axis=1)
    flags = jnp.concatenate([block[:, OFF : OFF + slots] for block in blocks], axis=1)
    first_row = lax.broadcasted_iota(jnp.int32, flags.shape, 0) == 0
    flags = jnp.where(first_row, flags, 0.0)
    field_high = fields.astype(BF16).astype(F32)
    left = jnp.concatenate([field_high, flags, fields - field_high, jnp.zeros_like(flags)], axis=0)

    lane = lanes_of((8, width))
    row_of = lax.broadcasted_iota(jnp.int32, (8, width), 0)
    one_row = jnp.where(row_of == 0, 1.0, 0.0)
    none = jnp.zeros((8, width), F32)
    spread = none
    for k in range(8):
        spread = jnp.where(row_of == k, jnp.broadcast_to(diffusivity[:, k : k + 1], (8, width)), spread)
    lines = [state[pl.ds(y, 8, stride=rows), :] for y in range(rows)]

    def advance(y, sums):
        forcing = sums[0:8] / jnp.maximum(jnp.broadcast_to(sums[8:9], (8, width)), 1.0)
        here = lines[y]
        north = lines[y + 1] if y + 1 < rows else north_edge
        south = lines[y - 1] if y > 0 else south_edge
        east = pltpu.roll(here, width - 1, 1)
        east = jnp.where(lane == width - 1, jnp.broadcast_to(east_edge[:, y : y + 1], (8, width)), east)
        west = pltpu.roll(here, 1, 1)
        west = jnp.where(lane == 0, jnp.broadcast_to(west_edge[:, y : y + 1], (8, width)), west)
        laplace = east + west + north + south - 4.0 * here
        along = jnp.broadcast_to(velocity[0, y : y + 1, :], (8, width))
        across = jnp.broadcast_to(velocity[1, y : y + 1, :], (8, width))
        advect = 0.5 * (along * (east - west) + across * (north - south))
        mask = jnp.broadcast_to(wet[y : y + 1, :], (8, width)).astype(F32)
        fresh = here + mask * (spread * laplace - advect + forcing)
        new_state[pl.ds(y, 8, stride=rows), :] = fresh
        seen = fresh * mask
        seen_high = seen.astype(BF16).astype(F32)
        return [seen_high, one_row, seen - seen_high, none]

    seen = []
    for y in range(WIN_R):
        moved = jnp.broadcast_to(late[y : y + 1, :], left.shape) > 0
        both = jnp.concatenate([jnp.where(moved, 0.0, left), jnp.where(moved, left, 0.0)], axis=0)
        sums = jnp.dot(
            both.astype(BF16), matrix[:, 2 * y * width : 2 * (y + 1) * width], preferred_element_type=F32
        )
        sums = sums[:, 0:width] + sums[:, width:]
        lines_seen = advance(y, sums[0:16] + sums[16:32])
        lines_seen += advance(y + WIN_R, sums[32:48] + sums[48:64])
        seen.append(jnp.concatenate(lines_seen, axis=0).astype(BF16))
    back = jnp.zeros((16, matrix.shape[0]), F32)
    for y in range(WIN_R):
        moved = jnp.broadcast_to(late[y : y + 1, :], back.shape) > 0
        part = lax.dot_general(
            jnp.concatenate([seen[y], seen[y]], axis=1), matrix[:, 2 * y * width : 2 * (y + 1) * width],
            NT, preferred_element_type=F32,
        )
        back = back + jnp.where(moved, part[32:48] + part[48:64], part[0:16] + part[16:32])
    pad = jnp.zeros((8, OFF - slots), F32)
    out = []
    for i in range(9):
        at = slice(i * slots, (i + 1) * slots)
        out.append(jnp.concatenate([back[0:8, at], pad, back[8:16, at], pad], axis=1))
    for q in range(3):
        up, down = out[6 + q], out[q]
        send1[q] = jnp.where(plus_r, up, down)
        send2[q] = jnp.where(plus_r, down, up)
        back_own[q] = out[3 + q]


def surface_kernel(row1, row2, col1, col2, own, hot, result):
    cells = result.shape[1]
    plus_r = far_is_plus("row")
    plus_c = far_is_plus("col")
    middle = [
        jnp.where(plus_r, row2[1], row1[1]),
        own[1],
        jnp.where(plus_r, row1[1], row2[1]),
    ]
    blocks = []
    for a in range(3):
        blocks += [
            jnp.where(plus_c, col2[a], col1[a]),
            middle[a],
            jnp.where(plus_c, col1[a], col2[a]),
        ]
    values = jnp.concatenate(blocks, axis=1)
    value_high = values.astype(BF16).astype(F32)
    left = jnp.concatenate([value_high, values - value_high], axis=0).astype(BF16)
    total = jnp.dot(left, hot[...], preferred_element_type=F32)
    total = total[0:8] + total[8:16]
    half = total.shape[1] // 2
    cover = jnp.maximum(jnp.broadcast_to(total[0:1, half : half + cells], (8, cells)), 1.0)
    result[...] = total[:, 0:cells] / cover


def swaps(count):
    near = [(i, i ^ 1) for i in range(count)]
    far = [(i, i + 1) for i in range(1, count - 1, 2)]
    far = far + [(j, i) for i, j in far]
    return near, far


def exchange(send1, send2, axis):
    near, far = swaps(lax.axis_size(axis))
    one = lax.ppermute(send1, axis, far)
    send2, _ = lax.optimization_barrier((send2, send1))
    two = lax.ppermute(send2, axis, near)
    return one, two


def column_sends(row1, row2, own, extra, plus_r, plus_c):
    minus = jnp.where(plus_r, row2, row1)
    plus = jnp.where(plus_r, row1, row2)
    low = jnp.stack([minus[0], own[0], plus[0]] + [edge for edge in extra[:1]])
    high = jnp.stack([minus[2], own[2], plus[2]] + [edge for edge in extra[1:]])
    return jnp.where(plus_c, high, low), jnp.where(plus_c, low, high)


def in_hbm(array):
    return pltpu.with_memory_space_constraint(array, pltpu.HBM)


def call(kernel, outs, scratch, specs, flops, size, *args, name, out_specs=None):
    return pl.pallas_call(
        kernel,
        out_shape=outs,
        in_specs=specs,
        out_specs=out_specs or [VMEM] * len(outs),
        scratch_shapes=scratch,
        compiler_params=pltpu.CompilerParams(vmem_limit_bytes=24 * 1024 * 1024),
        cost_estimate=pl.CostEstimate(flops=flops, bytes_accessed=size, transcendentals=0),
        name=name,
    )(*args)


def on_device(
    atm_flux,
    send_index,
    send_count,
    block_start,
    remap_weight,
    coupling,
    ocean_state,
    velocity,
    diffusivity,
    wet_mask,
):
    fields, rows, width = ocean_state.shape
    slots = send_index.shape[3]
    cells = rows * width
    atm_cells = atm_flux.shape[1]
    plus_r = far_is_plus("row")
    plus_c = far_is_plus("col")
    state = ocean_state.reshape(fields * rows, width)
    index = send_index.reshape(9, 1, slots)
    count = send_count.reshape(3, 1, 3)
    start = block_start.reshape(9, 1, slots)

    def shape(*dims, dtype=F32):
        return jax.ShapeDtypeStruct(dims, dtype)

    kept = [index, count, state, start, remap_weight, velocity, diffusivity.reshape(1, -1), wet_mask]
    send1, send2, own, index, count, state, start, weight, velocity, diffusivity, wet = call(
        pack_kernel,
        [shape(4, 8, width), shape(4, 8, width), shape(5, 8, width)]
        + [shape(*array.shape, dtype=array.dtype) for array in kept],
        [
            pltpu.VMEM(atm_flux.shape, F32),
            pltpu.VMEM(coupling.shape, F32),
            pltpu.VMEM((16, width), jnp.int32),
            pltpu.VMEM((8, width), F32),
            pltpu.SemaphoreType.DMA((10,)),
        ],
        [HBM] * 10,
        100_000, 1_000_000,
        *(in_hbm(array) for array in (atm_flux, index, count, coupling)),
        *(in_hbm(array) for array in kept[2:]),
        name="pack",
    )

    def spread(after):
        return call(
            spread_kernel,
            [shape(9 * slots, cells, dtype=BF16), shape(WIN_R, 9 * slots)],
            [pltpu.VMEM((16, width), F32)],
            [VMEM, VMEM, VMEM],
            20_000_000, 4_000_000,
            start, weight, after,
            name="spread",
        )

    row1, row2 = exchange(send1, send2, "row")
    send1, send2 = column_sends(row1, row2, own, [own[3], own[4]], plus_r, plus_c)
    col1, col2 = exchange(send1, send2, "col")
    matrix, late = spread(send1)
    fresh, send1, send2, own = call(
        ocean_kernel,
        [shape(fields * rows, width), shape(3, 8, width), shape(3, 8, width), shape(3, 8, width)],
        [],
        [VMEM] * 11,
        100_000_000, 4_000_000,
        row1, row2, col1, col2, own, matrix, late, state, velocity, diffusivity, wet,
        name="ocean",
    )
    row1, row2 = exchange(send1, send2, "row")
    send1, send2 = column_sends(row1, row2, own, [], plus_r, plus_c)
    col1, col2 = exchange(send1, send2, "col")
    hot, new_state = call(
        hot_kernel,
        [shape(9 * width, 2 * width, dtype=BF16), shape(fields * rows, width)],
        [pltpu.VMEM((16, width), jnp.int32), pltpu.SemaphoreType.DMA],
        [VMEM] * 4,
        1_000_000, 200_000,
        index, count, fresh, send1,
        out_specs=[VMEM, HBM],
        name="hot",
    )
    (result,) = call(
        surface_kernel,
        [shape(fields, atm_cells)],
        [],
        [VMEM] * 6,
        1_000_000, 200_000,
        row1, row2, col1, col2, own, hot,
        name="surface",
    )
    return new_state.reshape(ocean_state.shape), result


def solution(mesh):
    return jax.shard_map(
        on_device,
        mesh=mesh,
        in_specs=(
            P(None, ("row", "col")),
            P(("row", "col"), None, None, None),
            P(("row", "col"), None, None),
            P(("row", "col"), None, None, None),
            P(("row", "col"), None, None, None, None),
            P(),
            P(None, "row", "col"),
            P(None, "row", "col"),
            P(),
            P("row", "col"),
        ),
        out_specs=(P(None, "row", "col"), P(None, ("row", "col"))),
        check_vma=False,
    )
```
